32 devices in a mesh: groups: 2 (over y), gx: 16 (over z, x, core).
Axes of the slice: x: 2, y: 2, z: 4, core: 2. Of those that a mesh axis runs over, the one named last changes fastest.
Arguments:
- populations: float32 [19, 128, 8192], P(None, ('groups', 'gx')), parts along dimension 1, as said below
- relax_class: int32 [128, 8192], P(('groups', 'gx')), parts along dimension 0, may hold values from 0 to 3
- cotangent: float32 [19, 128, 8192], P(None, ('groups', 'gx')), parts along dimension 1, may hold values from -6 to 6
Outputs:
- final_populations: float32 [19, 128, 8192], P(None, ('groups', 'gx')), parts along dimension 1
- initial_gradient: float32 [19, 128, 8192], P(None, ('groups', 'gx')), parts along dimension 1
The draws below stay inside these ranges and needn't reach their ends.
There are 2 independent parts, one for each index of `groups`. The reference program is written for one: setup_inputs(seed, part) draws one part's arguments, and reference() takes and returns one part's arrays. A program takes and returns all parts, laid end to end along the dimension named above; each array names one. Nothing has to cross between parts.
Inputs may be any that keep to these rules, and one draw needn't show every extreme that they name: populations in direction k lie between 0.5 w_k and 1.5 w_k, w_k the lattice weights.
All inputs are finite; a program needn't handle non-finite values.
Results may differ from the reference program's by a relative error of at most 0.0001.
Values sent between devices are 32-bit elements; how exact they have to be, the bound alone decides.
No kernel may reach another device: no remote copies, remote signals or barrier semaphores. Data moves between devices by JAX's collectives and lax.ppermute only.
A program may use at most 64 MiB of HBM per device.

```python
import jax
import jax.numpy as jnp
from jax import lax

NY = 128
NZ = 64
STEPS = 3
NX = 64


def draw_populations(key, part):
    key = jax.random.fold_in(key, 11)
    uniform_part = jax.random.uniform(key, (19, NX, NY * NZ), jnp.float32)
    factor = 0.5 + uniform_part
    weights = jnp.array([1.0 / 3.0] + [1.0 / 18.0] * 6 + [1.0 / 36.0] * 12, jnp.float32)
    return (weights[:, None, None] * factor).astype(jnp.float32)


def plant(entries, rng, least, high):
    place = [jax.random.randint(jax.random.fold_in(rng, axis), (), 0, length) for axis, length in enumerate(entries.shape)]
    longest = entries.shape.index(max(entries.shape))
    neighbour = place[:longest] + [(place[longest] + 1) % entries.shape[longest]] + place[longest + 1:]
    return entries.at[tuple(place)].set(least).at[tuple(neighbour)].set(high)


def block_levels(stream_key, dims, split, smallest, high):
    def one(dim, parts):
        steps = jax.random.uniform(jax.random.fold_in(jax.random.fold_in(stream_key, 6), dim), (parts,), jnp.float32, smallest / len(split), high / len(split))
        return jnp.repeat(jnp.exp(steps), dims[dim] // parts).reshape((-1,) + (1,) * (len(dims) - dim - 1))

    level = one(*split[0])
    for cut in split[1:]:
        level = level * one(*cut)
    return level


def noise(stream_key, dims, spread, most, pieces=(), held_as=jnp.bfloat16):
    factor_of = block_levels(stream_key, dims, pieces, -0.22, 0.18) if pieces else 1.0
    values = jax.random.normal(stream_key, dims, jnp.float32) * spread * factor_of
    return jnp.minimum(jnp.maximum(values, -most), most).astype(held_as)


def setup_inputs(seed: int = 0, part: int = 0) -> dict:
    streams_of = jax.random.split(jax.random.key(seed), 4)
    part_splits = jax.random.split(jax.random.fold_in(streams_of[3], part), 4)
    return {
        "populations": draw_populations(jax.random.fold_in(jax.random.fold_in(streams_of[3], part), 71), part),
        "relax_class": plant(jax.random.randint(part_splits[1], (NX, NY * NZ), 0, 4), jax.random.fold_in(part_splits[1], 1), 0, 3).astype(jnp.int32),
        "cotangent": noise(part_splits[2], (19, NX, NY * NZ), 1.0, 6.0, ((1, 16),), jnp.float32),
    }


lattice_speeds = [(0, 0, 0), (1, 0, 0), (-1, 0, 0), (0, 1, 0), (0, -1, 0), (0, 0, 1), (0, 0, -1), (1, 1, 0), (-1, -1, 0), (1, -1, 0), (-1, 1, 0), (1, 0, 1), (-1, 0, -1), (1, 0, -1), (-1, 0, 1), (0, 1, 1), (0, -1, -1), (0, 1, -1), (0, -1, 1)]
lattice_weights = [1.0 / 3.0] + [1.0 / 18.0] * 6 + [1.0 / 36.0] * 12
relax_times = [1.0, 1.25, 1.6, 2.4]

def relax_rates(relax_class):
    rates = jnp.zeros(relax_class.shape, jnp.float32)
    for entry in range(4):
        rates = rates + jnp.where(relax_class == entry, 1.0 / relax_times[entry], 0.0).astype(jnp.float32)
    return rates

def collide(pops, omega):
    density = lax.optimization_barrier(jnp.sum(pops, axis=0))
    flows = []
    for axis_num in range(3):
        total = jnp.zeros(density.shape, jnp.float32)
        for entry in range(19):
            speed = lattice_speeds[entry][axis_num]
            if speed != 0:
                total = total + float(speed) * pops[entry]
        flows.append(total / density)
    usquare = flows[0] * flows[0] + flows[1] * flows[1] + flows[2] * flows[2]
    result = []
    for entry in range(19):
        along = jnp.zeros(density.shape, jnp.float32)
        for axis_num in range(3):
            speed = lattice_speeds[entry][axis_num]
            if speed != 0:
                along = along + float(speed) * flows[axis_num]
        equil = lattice_weights[entry] * density * (1.0 + 3.0 * along + 4.5 * along * along - 1.5 * usquare)
        result.append(pops[entry] + omega * (equil - pops[entry]))
    return jnp.stack(result)

def single_step(pops, omega):
    post = collide(pops, omega)
    moved = [jnp.roll(post[entry], lattice_speeds[entry], axis=(0, 1, 2)) for entry in range(19)]
    return jnp.stack(moved)

def reference(populations, relax_class, cotangent):
    shape_four = (19, populations.shape[1], NY, NZ)
    start = populations.reshape(shape_four)
    omega = relax_rates(relax_class).reshape(shape_four[1:])

    def forward(pops):
        for number in range(STEPS):
            pops = single_step(pops, omega)
        return pops
    final, pullback = jax.vjp(forward, start)
    gradient = pullback(cotangent.reshape(shape_four))[0]
    return (final.reshape(populations.shape), gradient.reshape(populations.shape))
```

```python
import jax
import jax.numpy as jnp
from jax import lax
from jax.experimental import pallas as pl
from jax.experimental.pallas import tpu as pltpu
from jax.sharding import PartitionSpec as P

PLANES, ROWS, LANES, BLOCKS = 4, 64, 128, 8
SPEEDS = [
    (0, 0, 0), (1, 0, 0), (-1, 0, 0), (0, 1, 0), (0, -1, 0), (0, 0, 1), (0, 0, -1),
    (1, 1, 0), (-1, -1, 0), (1, -1, 0), (-1, 1, 0), (1, 0, 1), (-1, 0, -1),
    (1, 0, -1), (-1, 0, 1), (0, 1, 1), (0, -1, -1), (0, 1, -1), (0, -1, 1),
]
RATES = [1.0 / 1.0, 1.0 / 1.25, 1.0 / 1.6, 1.0 / 2.4]
MIRROR = [SPEEDS.index((-cx, cy, cz)) for cx, cy, cz in SPEEDS]
PLUS = [k for k in range(19) if SPEEDS[k][0] == 1]
MINUS = [MIRROR[k] for k in PLUS]
F32 = jnp.float32


def iotas():
    lane = lax.broadcasted_iota(jnp.int32, (8, LANES), 1)
    row = lax.broadcasted_iota(jnp.int32, (8, LANES), 0)
    return {"high": lane >= 64, "first": lane % 64 == 0, "last": lane % 64 == 63,
            "top": row == 0, "bottom": row == 7}


def block(r):
    return pl.ds(pl.multiple_of(r * 8, 8), 8)


def shifted(ref, index, r, cy, cz, m):
    here = ref[index + (block(r), slice(None))]
    turn = 0
    if cy == 1:
        edge = ref[index + (pl.ds(lax.rem(r + 7, 8) * 8 + 7, 1), slice(None))]
        other = jnp.where(m["top"], edge, pltpu.roll(here, 1, 0))
        here, turn = jnp.where(m["high"], other, here), 64
    elif cy == -1:
        edge = ref[index + (pl.ds(lax.rem(r + 1, 8) * 8, 1), slice(None))]
        other = jnp.where(m["bottom"], edge, pltpu.roll(here, 7, 0))
        here, turn = jnp.where(m["high"], here, other), 64
    if cz == 0:
        return pltpu.roll(here, turn, 1) if turn else here
    main = pltpu.roll(here, (turn + cz) % LANES, 1)
    wrapped = pltpu.roll(here, (turn + cz + 64) % LANES, 1)
    return jnp.where(m["first"] if cz == 1 else m["last"], wrapped, main)


def moments(f):
    s = [f[k] + f[k + 1] for k in range(1, 19, 2)]
    d = [f[k] - f[k + 1] for k in range(1, 19, 2)]
    rho = f[0] + ((s[0] + s[1]) + (s[2] + s[3])) + ((s[4] + s[5]) + (s[6] + s[7])) + s[8]
    jx = d[0] + ((d[3] + d[4]) + (d[5] + d[6]))
    jy = d[1] + ((d[3] - d[4]) + (d[7] + d[8]))
    jz = d[2] + ((d[5] - d[6]) + (d[7] - d[8]))
    return rho, jx, jy, jz


def along(k, v):
    total = None
    for c, x in zip(SPEEDS[k], v):
        if c:
            x = x if c == 1 else -x
            total = x if total is None else (total + x)
    return total


def along_odd(k, v):
    total = None
    for c, x in zip(SPEEDS[k], v):
        if c:
            total = x if total is None else (total + x if c == 1 else total - x)
    return total


def relaxed(f, rho, u, om):
    keep = 1.0 - om
    wr = om * rho
    shape = 1.0 - 1.5 * (u[0] * u[0] + u[1] * u[1] + u[2] * u[2])
    out = [None] * 19
    out[0] = keep * f[0] + (wr * (1.0 / 3.0)) * shape
    for first, last, w in ((1, 7, 1.0 / 18.0), (7, 19, 1.0 / 36.0)):
        part = wr * w
        base, lin, quad = part * shape, part * 3.0, part * 4.5
        for k in range(first, last, 2):
            a = along_odd(k, u)
            even, odd = base + quad * (a * a), lin * a
            out[k] = keep * f[k] + (even + odd)
            out[k + 1] = keep * f[k + 1] + (even - odd)
    return out


def adjoint(mu, u, om):
    s = [None] + [mu[k] + mu[k + 1] for k in range(1, 19, 2)]
    d = [None] + [mu[k] - mu[k + 1] for k in range(1, 19, 2)]
    a, b = 1.0 / 18.0, 1.0 / 36.0
    s45, s67, s89 = s[4] + s[5], s[6] + s[7], s[8] + s[9]
    xx = a * s[1] + b * (s45 + s67)
    yy = a * s[2] + b * (s45 + s89)
    zz = a * s[3] + b * (s67 + s89)
    m0 = (1.0 / 3.0) * mu[0] + a * ((s[1] + s[2]) + s[3]) + b * ((s45 + s67) + s89)
    xy, xz, yz = b * (s[4] - s[5]), b * (s[6] - s[7]), b * (s[8] - s[9])
    mx = a * d[1] + b * ((d[4] + d[5]) + (d[6] + d[7]))
    my = a * d[2] + b * ((d[4] - d[5]) + (d[8] + d[9]))
    mz = a * d[3] + b * ((d[6] - d[7]) + (d[8] - d[9]))
    vx = xx * u[0] + xy * u[1] + xz * u[2]
    vy = xy * u[0] + yy * u[1] + yz * u[2]
    vz = xz * u[0] + yz * u[1] + zz * u[2]
    uu = u[0] * u[0] + u[1] * u[1] + u[2] * u[2]
    rho_part = om * (m0 + 1.5 * (m0 * uu) - 4.5 * (u[0] * vx + u[1] * vy + u[2] * vz))
    om3 = 3.0 * om
    flow = [
        om3 * (mx + 3.0 * vx - u[0] * m0),
        om3 * (my + 3.0 * vy - u[1] * m0),
        om3 * (mz + 3.0 * vz - u[2] * m0),
    ]
    keep = 1.0 - om
    out = [None] * 19
    out[0] = keep * mu[0] + rho_part
    for k in range(1, 19, 2):
        g = along_odd(k, flow)
        out[k] = keep * mu[k] + (rho_part + g)
        out[k + 1] = keep * mu[k + 1] + (rho_part - g)
    return out


def pulled(own, far, near, p, r, sign, m):
    plus, minus = (PLUS, MINUS) if sign == 1 else (MINUS, PLUS)
    out = []
    for k in range(19):
        cx, cy, cz = (sign * c for c in SPEEDS[k])
        source = p - cx
        if source < 0:
            out.append(shifted(far, (plus.index(k),), r, cy, cz, m))
        elif source >= PLANES:
            out.append(shifted(near, (minus.index(k),), r, cy, cz, m))
        else:
            out.append(shifted(own, (k, source), r, cy, cz, m))
    return out


def put_edges(values, p, r, far_ref, near_ref, far_set, near_set, offset=0):
    if p == 0:
        for i, k in enumerate(far_set):
            far_ref[offset + i, block(r), :] = values[k]
    if p == PLANES - 1:
        for i, k in enumerate(near_set):
            near_ref[offset + i, block(r), :] = values[k]


def native(flip, k, p, r):
    kk = k if MIRROR[k] == k else jnp.where(flip == 1, MIRROR[k], k)
    x = jnp.where(flip == 1, PLANES - 1 - p, p)
    return kk, pl.ds(r * (8 * PLANES) + x, 8, stride=PLANES)


def loop(body):
    lax.fori_loop(0, BLOCKS, lambda r, c: (body(r), c)[1], 0)


def chunk(ref, r):
    rows = 8 * PLANES
    return ref.at[:, pl.ds(pl.multiple_of(r * rows, rows), rows), :]


def copy_in(hbm, vmem, sem, r):
    return pltpu.make_async_copy(chunk(hbm, r), chunk(vmem, r), sem.at[r])


def flipped():
    return lax.rem(lax.axis_index("gx"), 2)


def put_velocity(u_ref, u, p, r):
    for i in range(3):
        u_ref[i, p, block(r), :] = u[i]


def get_velocity(u_ref, p, r):
    return [u_ref[i, p, block(r), :] for i in range(3)]


def collide_first(pops, classes, post, u0, om_ref, far_out, near_out, hold, sem):
    flip = flipped()
    loop(lambda r: copy_in(pops, hold, sem, r).start())

    def body(r):
        copy_in(pops, hold, sem, r).wait()
        for p in range(PLANES):
            f = []
            for k in range(19):
                kk, rows = native(flip, k, p, r)
                f.append(hold[kk, rows, :])
            cls = classes[native(flip, 0, p, r)[1], :]
            om = jnp.zeros((8, LANES), F32)
            for entry in range(4):
                om = jnp.where(cls == entry, RATES[entry], om)
            om_ref[p, block(r), :] = om
            rho, jx, jy, jz = moments(f)
            inv = 1.0 / rho
            u = [jx * inv, jy * inv, jz * inv]
            put_velocity(u0, u, p, r)
            out = relaxed(f, rho, u, om)
            for k in range(19):
                post[k, p, block(r), :] = out[k]
            put_edges(out, p, r, far_out, near_out, MINUS, PLUS)

    loop(body)


def canonical_cotangent(cot, own, far_out, near_out):
    flip = flipped()

    def body(r):
        for p in range(PLANES):
            values = []
            for k in range(19):
                kk, rows = native(flip, k, p, r)
                values.append(cot[kk, rows, :])
                own[k, p, block(r), :] = values[k]
            put_edges(values, p, r, far_out, near_out, PLUS, MINUS)

    loop(body)


def forward_step(own, far, near, om_ref, post, u_ref, far_out, near_out):
    m = iotas()

    def body(r):
        for p in range(PLANES):
            f = pulled(own, far, near, p, r, 1, m)
            rho, jx, jy, jz = moments(f)
            inv = 1.0 / rho
            u = [jx * inv, jy * inv, jz * inv]
            put_velocity(u_ref, u, p, r)
            out = relaxed(f, rho, u, om_ref[p, block(r), :])
            for k in range(19):
                post[k, p, block(r), :] = out[k]
            put_edges(out, p, r, far_out, near_out, MINUS, PLUS)

    loop(body)


def adjoint_step(own, far, near, om_ref, u_ref, lam, far_out, near_out):
    m = iotas()

    def body(r):
        for p in range(PLANES):
            mu = pulled(own, far, near, p, r, -1, m)
            out = adjoint(mu, get_velocity(u_ref, p, r), om_ref[p, block(r), :])
            for k in range(19):
                lam[k, p, block(r), :] = out[k]
            put_edges(out, p, r, far_out, near_out, PLUS, MINUS)

    loop(body)


def stream_last(own, far, near, final, hold, sem):
    flip, m = flipped(), iotas()

    def body(r):
        for p in range(PLANES):
            f = pulled(own, far, near, p, r, 1, m)
            for k in range(19):
                kk, rows = native(flip, k, p, r)
                hold[kk, rows, :] = f[k]
        pltpu.make_async_copy(chunk(hold, r), chunk(final, r), sem.at[r]).start()

    loop(body)
    loop(lambda r: pltpu.make_async_copy(chunk(hold, r), chunk(final, r), sem.at[r]).wait())


def adjoint_last(own, far, near, om_ref, u_ref, grad, hold, sem):
    flip, m = flipped(), iotas()

    def body(r):
        for p in range(PLANES):
            mu = pulled(own, far, near, p, r, -1, m)
            out = adjoint(mu, get_velocity(u_ref, p, r), om_ref[p, block(r), :])
            for k in range(19):
                kk, rows = native(flip, k, p, r)
                hold[kk, rows, :] = out[k]
        pltpu.make_async_copy(chunk(hold, r), chunk(grad, r), sem.at[r]).start()

    loop(body)
    loop(lambda r: pltpu.make_async_copy(chunk(hold, r), chunk(grad, r), sem.at[r]).wait())


INSIDE = pl.BlockSpec(memory_space=pltpu.VMEM)
OUTSIDE = pl.BlockSpec(memory_space=pltpu.HBM)
FULL = (19, PLANES, ROWS, LANES)
VELOCITY = (3, PLANES, ROWS, LANES)
RELAX = (PLANES, ROWS, LANES)
EDGE = (5, ROWS, LANES)
NATIVE = (19, PLANES * ROWS, LANES)
STAGED = [pltpu.VMEM(NATIVE, F32), pltpu.SemaphoreType.DMA((BLOCKS,))]


def kernel(body, outs, scratch=(), flops=0):
    def call(*args):
        specs = [INSIDE if inside else OUTSIDE for _, inside in args]
        args = [
            pltpu.with_memory_space_constraint(x, pltpu.VMEM if inside else pltpu.HBM)
            for x, inside in args
        ]
        return pl.pallas_call(
            body,
            in_specs=specs,
            out_specs=[INSIDE if inside else OUTSIDE for _, inside in outs],
            out_shape=[
                pltpu.VMEM(s, F32) if inside else jax.ShapeDtypeStruct(s, F32) for s, inside in outs
            ],
            scratch_shapes=list(scratch),
            compiler_params=pltpu.CompilerParams(vmem_limit_bytes=16 * 2**20),
        )(*args)

    return call


def local(populations, relax_class, cotangent):
    count = lax.axis_size("gx")
    near_pairs = [(i, i ^ 1) for i in range(count)]
    far_pairs = [(i, (i + 1 if i % 2 else i - 1) % count) for i in range(count)]

    def exchange(far, near):
        return lax.ppermute(far, "gx", far_pairs), lax.ppermute(near, "gx", near_pairs)

    def to_native(x):
        lead = x.shape[:-2]
        x = x.reshape(lead + (PLANES, ROWS, LANES))
        return jnp.swapaxes(x, -3, -2).reshape(lead + (PLANES * ROWS, LANES))

    def from_native(x):
        return jnp.swapaxes(x.reshape(19, ROWS, PLANES, LANES), 1, 2).reshape(populations.shape)

    pops, classes, cot = to_native(populations), to_native(relax_class), to_native(cotangent)
    edges = [(EDGE, 1), (EDGE, 1)]
    post0, u0, om, far, near = kernel(
        collide_first, [(FULL, 1), (VELOCITY, 1), (RELAX, 1)] + edges, STAGED
    )((pops, 0), (classes, 1))
    far0, near0 = exchange(far, near)
    lam3, far, near = kernel(canonical_cotangent, [(FULL, 1)] + edges)((cot, 1))
    farc, nearc = exchange(far, near)
    step = kernel(forward_step, [(FULL, 1), (VELOCITY, 1)] + edges)
    back = kernel(adjoint_step, [(FULL, 1)] + edges)
    post1, u1, far, near = step((post0, 1), (far0, 1), (near0, 1), (om, 1))
    far1, near1 = exchange(far, near)
    post2, u2, far, near = step((post1, 1), (far1, 1), (near1, 1), (om, 1))
    far2, near2 = exchange(far, near)
    lam2, far, near = back((lam3, 1), (farc, 1), (nearc, 1), (om, 1), (u2, 1))
    farb, nearb = exchange(far, near)
    lam1, far, near = back((lam2, 1), (farb, 1), (nearb, 1), (om, 1), (u1, 1))
    fara, neara = exchange(far, near)
    (final,) = kernel(stream_last, [(NATIVE, 0)], STAGED)((post2, 1), (far2, 1), (near2, 1))
    (grad,) = kernel(adjoint_last, [(NATIVE, 0)], STAGED)(
        (lam1, 1), (fara, 1), (neara, 1), (om, 1), (u0, 1)
    )
    return from_native(final), from_native(grad)


def solution(mesh):
    return jax.shard_map(
        local,
        mesh=mesh,
        in_specs=(
            P(None, ("groups", "gx"), None),
            P(("groups", "gx"), None),
            P(None, ("groups", "gx"), None),
        ),
        out_specs=(P(None, ("groups", "gx"), None), P(None, ("groups", "gx"), None)),
        check_vma=False,
    )
```

```python
import jax
import jax.numpy as jnp
from jax import lax
from jax.experimental import pallas as pl
from jax.experimental.pallas import tpu as pltpu
from jax.sharding import PartitionSpec as P

PLANES, ROWS, LANES, BLOCKS = 4, 64, 128, 8
SPEEDS = [
    (0, 0, 0), (1, 0, 0), (-1, 0, 0), (0, 1, 0), (0, -1, 0), (0, 0, 1), (0, 0, -1),
    (1, 1, 0), (-1, -1, 0), (1, -1, 0), (-1, 1, 0), (1, 0, 1), (-1, 0, -1),
    (1, 0, -1), (-1, 0, 1), (0, 1, 1), (0, -1, -1), (0, 1, -1), (0, -1, 1),
]
RATES = [1.0 / 1.0, 1.0 / 1.25, 1.0 / 1.6, 1.0 / 2.4]
MIRROR = [SPEEDS.index((-cx, cy, cz)) for cx, cy, cz in SPEEDS]
PLUS = [k for k in range(19) if SPEEDS[k][0] == 1]
MINUS = [MIRROR[k] for k in PLUS]
F32 = jnp.float32


def iotas():
    lane = lax.broadcasted_iota(jnp.int32, (8, LANES), 1)
    row = lax.broadcasted_iota(jnp.int32, (8, LANES), 0)
    return {"high": lane >= 64, "first": lane % 64 == 0, "last": lane % 64 == 63,
            "top": row == 0, "bottom": row == 7}


def block(r):
    return pl.ds(pl.multiple_of(r * 8, 8), 8)


def shifted(ref, index, r, cy, cz, m):
    here = ref[index + (block(r), slice(None))]
    turn = 0
    if cy == 1:
        edge = ref[index + (pl.ds(lax.rem(r + 7, 8) * 8 + 7, 1), slice(None))]
        other = jnp.where(m["top"], edge, pltpu.roll(here, 1, 0))
        here, turn = jnp.where(m["high"], other, here), 64
    elif cy == -1:
        edge = ref[index + (pl.ds(lax.rem(r + 1, 8) * 8, 1), slice(None))]
        other = jnp.where(m["bottom"], edge, pltpu.roll(here, 7, 0))
        here, turn = jnp.where(m["high"], here, other), 64
    if cz == 0:
        return pltpu.roll(here, turn, 1) if turn else here
    main = pltpu.roll(here, (turn + cz) % LANES, 1)
    wrapped = pltpu.roll(here, (turn + cz + 64) % LANES, 1)
    return jnp.where(m["first"] if cz == 1 else m["last"], wrapped, main)


def moments(f):
    s = [f[k] + f[k + 1] for k in range(1, 19, 2)]
    d = [f[k] - f[k + 1] for k in range(1, 19, 2)]
    rho = f[0] + ((s[0] + s[1]) + (s[2] + s[3])) + ((s[4] + s[5]) + (s[6] + s[7])) + s[8]
    jx = d[0] + ((d[3] + d[4]) + (d[5] + d[6]))
    jy = d[1] + ((d[3] - d[4]) + (d[7] + d[8]))
    jz = d[2] + ((d[5] - d[6]) + (d[7] - d[8]))
    return rho, jx, jy, jz


def along_odd(k, v):
    total = None
    for c, x in zip(SPEEDS[k], v):
        if c:
            total = x if total is None else (total + x if c == 1 else total - x)
    return total


def relaxed(f, rho, u, om):
    keep = 1.0 - om
    wr = om * rho
    shape = 1.0 - 1.5 * (u[0] * u[0] + u[1] * u[1] + u[2] * u[2])
    out = [None] * 19
    out[0] = keep * f[0] + (wr * (1.0 / 3.0)) * shape
    for first, last, w in ((1, 7, 1.0 / 18.0), (7, 19, 1.0 / 36.0)):
        part = wr * w
        base, lin, quad = part * shape, part * 3.0, part * 4.5
        for k in range(first, last, 2):
            a = along_odd(k, u)
            even, odd = base + quad * (a * a), lin * a
            out[k] = keep * f[k] + (even + odd)
            out[k + 1] = keep * f[k + 1] + (even - odd)
    return out


def adjoint(mu, u, om):
    s = [None] + [mu[k] + mu[k + 1] for k in range(1, 19, 2)]
    d = [None] + [mu[k] - mu[k + 1] for k in range(1, 19, 2)]
    a, b = 1.0 / 18.0, 1.0 / 36.0
    s45, s67, s89 = s[4] + s[5], s[6] + s[7], s[8] + s[9]
    xx = a * s[1] + b * (s45 + s67)
    yy = a * s[2] + b * (s45 + s89)
    zz = a * s[3] + b * (s67 + s89)
    m0 = (1.0 / 3.0) * mu[0] + a * ((s[1] + s[2]) + s[3]) + b * ((s45 + s67) + s89)
    xy, xz, yz = b * (s[4] - s[5]), b * (s[6] - s[7]), b * (s[8] - s[9])
    mx = a * d[1] + b * ((d[4] + d[5]) + (d[6] + d[7]))
    my = a * d[2] + b * ((d[4] - d[5]) + (d[8] + d[9]))
    mz = a * d[3] + b * ((d[6] - d[7]) + (d[8] - d[9]))
    vx = xx * u[0] + xy * u[1] + xz * u[2]
    vy = xy * u[0] + yy * u[1] + yz * u[2]
    vz = xz * u[0] + yz * u[1] + zz * u[2]
    uu = u[0] * u[0] + u[1] * u[1] + u[2] * u[2]
    rho_part = om * (m0 + 1.5 * (m0 * uu) - 4.5 * (u[0] * vx + u[1] * vy + u[2] * vz))
    om3 = 3.0 * om
    flow = [
        om3 * (mx + 3.0 * vx - u[0] * m0),
        om3 * (my + 3.0 * vy - u[1] * m0),
        om3 * (mz + 3.0 * vz - u[2] * m0),
    ]
    keep = 1.0 - om
    out = [None] * 19
    out[0] = keep * mu[0] + rho_part
    for k in range(1, 19, 2):
        g = along_odd(k, flow)
        out[k] = keep * mu[k] + (rho_part + g)
        out[k + 1] = keep * mu[k + 1] + (rho_part - g)
    return out


EDGES, INNER = (0, PLANES - 1), (1, 2)


def plane_of(edge, inner, p):
    return (edge, EDGES.index(p)) if p in EDGES else (inner, INNER.index(p))


def pull_local(edge, inner, p, r, sign, m):
    out = [None] * 19
    for k in range(19):
        cx, cy, cz = (sign * c for c in SPEEDS[k])
        if 0 <= p - cx < PLANES:
            ref, i = plane_of(edge, inner, p - cx)
            out[k] = shifted(ref, (k, i), r, cy, cz, m)
    return out


def crossing(p, sign):
    return (PLUS, MINUS)[(sign == 1) != (p == 0)]


def pull_remote(other, out, p, r, sign, m):
    for i, k in enumerate(crossing(p, sign)):
        out[k] = shifted(other, (i,), r, sign * SPEEDS[k][1], sign * SPEEDS[k][2], m)
    return out


def put_all(ref, values, i, r):
    for k in range(19):
        if values[k] is not None:
            ref[k, i, block(r), :] = values[k]


def get_some(ref, i, r, missing=()):
    return [None if k in missing else ref[k, i, block(r), :] for k in range(19)]


def put_crossing(far_ref, near_ref, values, p, r, sign):
    ref = far_ref if p == 0 else near_ref
    for i, k in enumerate(crossing(p, -sign)):
        ref[i, block(r), :] = values[k]


def put_velocity(u_ref, u, i, r):
    for j in range(3):
        u_ref[j, i, block(r), :] = u[j]


def get_velocity(u_ref, i, r):
    return [u_ref[j, i, block(r), :] for j in range(3)]


def state_of(f):
    rho, jx, jy, jz = moments(f)
    inv = 1.0 / rho
    return rho, [jx * inv, jy * inv, jz * inv]


def native(flip, k, p, r):
    kk = k if MIRROR[k] == k else jnp.where(flip == 1, MIRROR[k], k)
    x = jnp.where(flip == 1, PLANES - 1 - p, p)
    return kk, pl.ds(r * (8 * PLANES) + x, 8, stride=PLANES)


def get_native(ref, flip, p, r):
    out = []
    for k in range(19):
        kk, rows = native(flip, k, p, r)
        out.append(ref[kk, rows, :])
    return out


def put_native(ref, values, flip, p, r):
    for k in range(19):
        kk, rows = native(flip, k, p, r)
        ref[kk, rows, :] = values[k]


def loop(body):
    lax.fori_loop(0, BLOCKS, lambda r, c: (body(r), c)[1], 0)


def chunk(ref, r):
    rows = 8 * PLANES
    return ref.at[:, pl.ds(pl.multiple_of(r * rows, rows), rows), :]


def moved(source, target, sem, r):
    return pltpu.make_async_copy(chunk(source, r), chunk(target, r), sem.at[r])


def flipped():
    return lax.rem(lax.axis_index("gx"), 2)


def first_edges(pops, classes, held, om_ref, post, u_ref, far_out, near_out, cls_ref, sem, cls_sem):
    flip = flipped()
    fetch = pltpu.make_async_copy(classes, cls_ref, cls_sem)
    fetch.start()
    loop(lambda r: moved(pops, held, sem, r).start())
    fetch.wait()

    def body(r):
        moved(pops, held, sem, r).wait()
        for p in range(PLANES):
            cls = cls_ref[native(flip, 0, p, r)[1], :]
            om = jnp.full((8, LANES), RATES[0], F32)
            for entry in range(1, 4):
                om = jnp.where(cls == entry, RATES[entry], om)
            om_ref[p, block(r), :] = om
            if p in EDGES:
                i = EDGES.index(p)
                f = get_native(held, flip, p, r)
                rho, u = state_of(f)
                put_velocity(u_ref, u, i, r)
                out = relaxed(f, rho, u, om)
                put_all(post, out, i, r)
                put_crossing(far_out, near_out, out, p, r, 1)

    loop(body)


def first_inner(held, om_ref, post, u_ref):
    flip = flipped()

    def body(r):
        for i, p in enumerate(INNER):
            f = get_native(held, flip, p, r)
            rho, u = state_of(f)
            put_velocity(u_ref, u, i, r)
            put_all(post, relaxed(f, rho, u, om_ref[p, block(r), :]), i, r)

    loop(body)


def cotangent_planes(cot, edge, inner, far_out, near_out):
    flip = flipped()

    def body(r):
        for p in range(PLANES):
            values = get_native(cot, flip, p, r)
            ref, i = plane_of(edge, inner, p)
            put_all(ref, values, i, r)
            if p in EDGES:
                put_crossing(far_out, near_out, values, p, r, -1)

    loop(body)


def forward_inner(edge, inner, om_ref, post, u_ref, ready):
    m = iotas()

    def body(r):
        for i, p in enumerate(INNER):
            f = pull_local(edge, inner, p, r, 1, m)
            rho, u = state_of(f)
            put_velocity(u_ref, u, i, r)
            put_all(post, relaxed(f, rho, u, om_ref[p, block(r), :]), i, r)
        for i, p in enumerate(EDGES):
            put_all(ready, pull_local(edge, inner, p, r, 1, m), i, r)

    loop(body)


def edge_values(ready, far, near, i, p, r, sign, m):
    values = get_some(ready, i, r, crossing(p, sign))
    return pull_remote(far if p == 0 else near, values, p, r, sign, m)


def forward_edges(ready, far, near, om_ref, post, u_ref, far_out, near_out):
    m = iotas()

    def body(r):
        for i, p in enumerate(EDGES):
            f = edge_values(ready, far, near, i, p, r, 1, m)
            rho, u = state_of(f)
            put_velocity(u_ref, u, i, r)
            out = relaxed(f, rho, u, om_ref[p, block(r), :])
            put_all(post, out, i, r)
            put_crossing(far_out, near_out, out, p, r, 1)

    loop(body)


def adjoint_inner(edge, inner, om_ref, u_ref, lam, ready):
    m = iotas()

    def body(r):
        for i, p in enumerate(INNER):
            mu = pull_local(edge, inner, p, r, -1, m)
            put_all(lam, adjoint(mu, get_velocity(u_ref, i, r), om_ref[p, block(r), :]), i, r)
        for i, p in enumerate(EDGES):
            put_all(ready, pull_local(edge, inner, p, r, -1, m), i, r)

    loop(body)


def adjoint_edges(ready, far, near, om_ref, u_ref, lam, far_out, near_out):
    m = iotas()

    def body(r):
        for i, p in enumerate(EDGES):
            mu = edge_values(ready, far, near, i, p, r, -1, m)
            out = adjoint(mu, get_velocity(u_ref, i, r), om_ref[p, block(r), :])
            put_all(lam, out, i, r)
            put_crossing(far_out, near_out, out, p, r, -1)

    loop(body)


def turn_edges(ready, far, near, om_ref, mus, farc, nearc, post, lam, far_post, near_post, far_out, near_out):
    m = iotas()

    def body(r):
        for i, p in enumerate(EDGES):
            om = om_ref[p, block(r), :]
            f = edge_values(ready, far, near, i, p, r, 1, m)
            rho, u = state_of(f)
            out = relaxed(f, rho, u, om)
            put_all(post, out, i, r)
            put_crossing(far_post, near_post, out, p, r, 1)
            out = adjoint(edge_values(mus, farc, nearc, i, p, r, -1, m), u, om)
            put_all(lam, out, i, r)
            put_crossing(far_out, near_out, out, p, r, -1)

    loop(body)


def stream_last(edge, inner, far, near, final, hold, sem):
    flip, m = flipped(), iotas()

    def body(r):
        for p in range(PLANES):
            f = pull_local(edge, inner, p, r, 1, m)
            if p in EDGES:
                pull_remote(far if p == 0 else near, f, p, r, 1, m)
            put_native(hold, f, flip, p, r)
        moved(hold, final, sem, r).start()

    loop(body)
    loop(lambda r: moved(hold, final, sem, r).wait())


def adjoint_last(ready, far, near, om_ref, u_ref, inner, grad, hold, sem):
    flip, m = flipped(), iotas()

    def body(r):
        for i, p in enumerate(EDGES):
            mu = edge_values(ready, far, near, i, p, r, -1, m)
            out = adjoint(mu, get_velocity(u_ref, i, r), om_ref[p, block(r), :])
            put_native(hold, out, flip, p, r)
        for i, p in enumerate(INNER):
            put_native(hold, get_some(inner, i, r), flip, p, r)
        moved(hold, grad, sem, r).start()

    loop(body)
    loop(lambda r: moved(hold, grad, sem, r).wait())


INSIDE = pl.BlockSpec(memory_space=pltpu.VMEM)
OUTSIDE = pl.BlockSpec(memory_space=pltpu.HBM)
PAIR = (19, 2, ROWS, LANES)
VELOCITY = (3, 2, ROWS, LANES)
RELAX = (PLANES, ROWS, LANES)
CROSS = (5, ROWS, LANES)
NATIVE = (19, PLANES * ROWS, LANES)
SEMS = pltpu.SemaphoreType.DMA((BLOCKS,))
STAGED = [pltpu.VMEM(NATIVE, F32), SEMS]


def kernel(body, outs, scratch=()):
    def call(*args):
        args = [x if isinstance(x, tuple) else (x, 1) for x in args]
        return pl.pallas_call(
            body,
            in_specs=[INSIDE if inside else OUTSIDE for _, inside in args],
            out_specs=[INSIDE if inside else OUTSIDE for _, inside in outs],
            out_shape=[
                pltpu.VMEM(s, F32) if inside else jax.ShapeDtypeStruct(s, F32) for s, inside in outs
            ],
            scratch_shapes=list(scratch),
            compiler_params=pltpu.CompilerParams(vmem_limit_bytes=8 * 2**20),
            name=body.__name__,
        )(
            *[
                pltpu.with_memory_space_constraint(x, pltpu.VMEM if inside else pltpu.HBM)
                for x, inside in args
            ]
        )

    return call


def local(populations, relax_class, cotangent):
    count = lax.axis_size("gx")
    near_pairs = [(i, i ^ 1) for i in range(count)]
    far_pairs = [(i, (i + 1 if i % 2 else i - 1) % count) for i in range(count)]

    def exchange(far, near):
        near = lax.ppermute(near, "gx", near_pairs)
        return lax.ppermute(far, "gx", far_pairs), near

    def to_native(x):
        lead = x.shape[:-2]
        x = x.reshape(lead + (PLANES, ROWS, LANES))
        return jnp.swapaxes(x, -3, -2).reshape(lead + (PLANES * ROWS, LANES))

    def from_native(x):
        return jnp.swapaxes(x.reshape(19, ROWS, PLANES, LANES), 1, 2).reshape(populations.shape)

    pops, classes, cot = to_native(populations), to_native(relax_class), to_native(cotangent)
    pair, speed, cross = (PAIR, 1), (VELOCITY, 1), (CROSS, 1)
    held, om, post_e, u0_e, far, near = kernel(
        first_edges,
        [(NATIVE, 1), (RELAX, 1), pair, speed, cross, cross],
        [pltpu.VMEM(classes.shape, jnp.int32), SEMS, pltpu.SemaphoreType.DMA],
    )((pops, 0), (classes, 0))
    far, near = exchange(far, near)
    post_i, u0_i = kernel(first_inner, [pair, speed])(held, om)
    cot_e, cot_i, farc, nearc = kernel(cotangent_planes, [pair, pair, cross, cross])(cot)
    farc, nearc = exchange(farc, nearc)
    inner = kernel(forward_inner, [pair, speed, pair])
    back_inner = kernel(adjoint_inner, [pair, pair])
    back_edges = kernel(adjoint_edges, [pair, cross, cross])

    post_i, u1_i, ready = inner(post_e, post_i, om)
    post_e, u1_e, far, near = kernel(forward_edges, [pair, speed, cross, cross])(ready, far, near, om)
    far, near = exchange(far, near)
    post_i, u2_i, ready = inner(post_e, post_i, om)
    lam_i, mus = back_inner(cot_e, cot_i, om, u2_i)
    post_e, lam_e, far_post, near_post, far, near = kernel(
        turn_edges, [pair, pair, cross, cross, cross, cross]
    )(ready, far, near, om, mus, farc, nearc)
    far, near = exchange(far, near)
    far_post, near_post = exchange(far_post, near_post)
    lam_i, ready = back_inner(lam_e, lam_i, om, u1_i)
    lam_e, far, near = back_edges(ready, far, near, om, u1_e)
    far, near = exchange(far, near)
    (final,) = kernel(stream_last, [(NATIVE, 0)], STAGED)(post_e, post_i, far_post, near_post)
    lam_i, ready = back_inner(lam_e, lam_i, om, u0_i)
    (grad,) = kernel(adjoint_last, [(NATIVE, 0)], STAGED)(ready, far, near, om, u0_e, lam_i)
    return from_native(final), from_native(grad)


def solution(mesh):
    return jax.shard_map(
        local,
        mesh=mesh,
        in_specs=(
            P(None, ("groups", "gx"), None),
            P(("groups", "gx"), None),
            P(None, ("groups", "gx"), None),
        ),
        out_specs=(P(None, ("groups", "gx"), None), P(None, ("groups", "gx"), None)),
        check_vma=False,
    )
```

```python
import jax
import jax.numpy as jnp
from jax import lax
from jax.experimental import pallas as pl
from jax.experimental.pallas import tpu as pltpu
from jax.sharding import PartitionSpec as P

PLANES, ROWS, LANES, BLOCKS = 4, 64, 128, 8
SPEEDS = [
    (0, 0, 0), (1, 0, 0), (-1, 0, 0), (0, 1, 0), (0, -1, 0), (0, 0, 1), (0, 0, -1),
    (1, 1, 0), (-1, -1, 0), (1, -1, 0), (-1, 1, 0), (1, 0, 1), (-1, 0, -1),
    (1, 0, -1), (-1, 0, 1), (0, 1, 1), (0, -1, -1), (0, 1, -1), (0, -1, 1),
]
RATES = [1.0 / 1.0, 1.0 / 1.25, 1.0 / 1.6, 1.0 / 2.4]
MIRROR = [SPEEDS.index((-cx, cy, cz)) for cx, cy, cz in SPEEDS]
PLUS = [k for k in range(19) if SPEEDS[k][0] == 1]
MINUS = [MIRROR[k] for k in PLUS]
F32 = jnp.float32


def iotas():
    lane = lax.broadcasted_iota(jnp.int32, (8, LANES), 1)
    row = lax.broadcasted_iota(jnp.int32, (8, LANES), 0)
    turns = {}
    for turn in (0, 64):
        for cz in (1, -1):
            turns[turn, cz] = ((lane & 64) ^ turn) | ((lane - cz) & 63)
    return {"high": lane >= 64, "top": row == 0, "bottom": row == 7, **turns}


def block(r):
    return pl.ds(r * 8 if isinstance(r, int) else pl.multiple_of(r * 8, 8), 8)


def shifted(ref, index, r, cy, cz, m):
    here = ref[index + (block(r), slice(None))]
    turn = 0
    if cy == 1:
        edge = ref[index + (pl.ds(((r + 7) & 7) * 8 + 7, 1), slice(None))]
        other = jnp.where(m["top"], edge, pltpu.roll(here, 1, 0))
        here, turn = jnp.where(m["high"], other, here), 64
    elif cy == -1:
        edge = ref[index + (pl.ds(((r + 1) & 7) * 8, 1), slice(None))]
        other = jnp.where(m["bottom"], edge, pltpu.roll(here, 7, 0))
        here, turn = jnp.where(m["high"], here, other), 64
    if cz == 0:
        return pltpu.roll(here, turn, 1) if turn else here
    return jnp.take_along_axis(here, m[turn, cz], axis=1)


def moments(f):
    s = [f[k] + f[k + 1] for k in range(1, 19, 2)]
    d = [f[k] - f[k + 1] for k in range(1, 19, 2)]
    rho = f[0] + ((s[0] + s[1]) + (s[2] + s[3])) + ((s[4] + s[5]) + (s[6] + s[7])) + s[8]
    jx = d[0] + ((d[3] + d[4]) + (d[5] + d[6]))
    jy = d[1] + ((d[3] - d[4]) + (d[7] + d[8]))
    jz = d[2] + ((d[5] - d[6]) + (d[7] - d[8]))
    return rho, jx, jy, jz


def along_odd(k, v):
    total = None
    for c, x in zip(SPEEDS[k], v):
        if c:
            total = x if total is None else (total + x if c == 1 else total - x)
    return total


def relaxed(f, rho, u, om):
    keep = 1.0 - om
    wr = om * rho
    shape = 1.0 - 1.5 * (u[0] * u[0] + u[1] * u[1] + u[2] * u[2])
    out = [None] * 19
    out[0] = keep * f[0] + (wr * (1.0 / 3.0)) * shape
    for first, last, w in ((1, 7, 1.0 / 18.0), (7, 19, 1.0 / 36.0)):
        part = wr * w
        base, lin, quad = part * shape, part * 3.0, part * 4.5
        for k in range(first, last, 2):
            a = along_odd(k, u)
            even, odd = base + quad * (a * a), lin * a
            out[k] = keep * f[k] + (even + odd)
            out[k + 1] = keep * f[k + 1] + (even - odd)
    return out


def adjoint(mu, u, om):
    s = [None] + [mu[k] + mu[k + 1] for k in range(1, 19, 2)]
    d = [None] + [mu[k] - mu[k + 1] for k in range(1, 19, 2)]
    a, b = 1.0 / 18.0, 1.0 / 36.0
    s45, s67, s89 = s[4] + s[5], s[6] + s[7], s[8] + s[9]
    xx = a * s[1] + b * (s45 + s67)
    yy = a * s[2] + b * (s45 + s89)
    zz = a * s[3] + b * (s67 + s89)
    m0 = (1.0 / 3.0) * mu[0] + a * ((s[1] + s[2]) + s[3]) + b * ((s45 + s67) + s89)
    xy, xz, yz = b * (s[4] - s[5]), b * (s[6] - s[7]), b * (s[8] - s[9])
    mx = a * d[1] + b * ((d[4] + d[5]) + (d[6] + d[7]))
    my = a * d[2] + b * ((d[4] - d[5]) + (d[8] + d[9]))
    mz = a * d[3] + b * ((d[6] - d[7]) + (d[8] - d[9]))
    vx = xx * u[0] + xy * u[1] + xz * u[2]
    vy = xy * u[0] + yy * u[1] + yz * u[2]
    vz = xz * u[0] + yz * u[1] + zz * u[2]
    uu = u[0] * u[0] + u[1] * u[1] + u[2] * u[2]
    rho_part = om * (m0 + 1.5 * (m0 * uu) - 4.5 * (u[0] * vx + u[1] * vy + u[2] * vz))
    om3 = 3.0 * om
    flow = [
        om3 * (mx + 3.0 * vx - u[0] * m0),
        om3 * (my + 3.0 * vy - u[1] * m0),
        om3 * (mz + 3.0 * vz - u[2] * m0),
    ]
    keep = 1.0 - om
    out = [None] * 19
    out[0] = keep * mu[0] + rho_part
    for k in range(1, 19, 2):
        g = along_odd(k, flow)
        out[k] = keep * mu[k] + (rho_part + g)
        out[k + 1] = keep * mu[k + 1] + (rho_part - g)
    return out


EDGES, INNER = (0, PLANES - 1), (1, 2)


def plane_of(edge, inner, p):
    return (edge, EDGES.index(p)) if p in EDGES else (inner, INNER.index(p))


def pull_local(edge, inner, p, r, sign, m):
    out = [None] * 19
    for k in range(19):
        cx, cy, cz = (sign * c for c in SPEEDS[k])
        if 0 <= p - cx < PLANES:
            ref, i = plane_of(edge, inner, p - cx)
            out[k] = shifted(ref, (k, i), r, cy, cz, m)
    return out


def crossing(p, sign):
    return (PLUS, MINUS)[(sign == 1) != (p == 0)]


def pull_remote(other, out, p, r, sign, m):
    for i, k in enumerate(crossing(p, sign)):
        out[k] = shifted(other, (i,), r, sign * SPEEDS[k][1], sign * SPEEDS[k][2], m)
    return out


def put_all(ref, values, i, r):
    for k in range(19):
        if values[k] is not None:
            ref[k, i, block(r), :] = values[k]


def get_some(ref, i, r, missing=()):
    return [None if k in missing else ref[k, i, block(r), :] for k in range(19)]


def put_crossing(far_ref, near_ref, values, p, r, sign):
    ref = far_ref if p == 0 else near_ref
    for i, k in enumerate(crossing(p, -sign)):
        ref[i, block(r), :] = values[k]


def put_velocity(u_ref, u, i, r):
    for j, value in enumerate(u):
        u_ref[j, i, block(r), :] = value


def get_velocity(u_ref, i, r):
    return [u_ref[j, i, block(r), :] for j in range(3)]


def state_of(f):
    rho, jx, jy, jz = moments(f)
    inv = 1.0 / rho
    return rho, [jx * inv, jy * inv, jz * inv]


def native(flip, k, p, r):
    kk = k if MIRROR[k] == k else jnp.where(flip == 1, MIRROR[k], k)
    x = jnp.where(flip == 1, PLANES - 1 - p, p)
    return kk, pl.ds(r * (8 * PLANES) + x, 8, stride=PLANES)


def get_native(ref, flip, p, r):
    out = []
    for k in range(19):
        kk, rows = native(flip, k, p, r)
        out.append(ref[kk, rows, :])
    return out


def loop(body):
    lax.fori_loop(0, BLOCKS, lambda r, c: (body(r), c)[1], 0)


def chunk(ref, r):
    rows = 8 * PLANES
    return ref.at[:, pl.ds(pl.multiple_of(r * rows, rows), rows), :]


def moved(source, target, sem, r):
    return pltpu.make_async_copy(chunk(source, r), chunk(target, r), sem.at[r])


def flipped():
    return lax.rem(lax.axis_index("gx"), 2)


def first_edges(pops, classes, held, om_ref, post, u_ref, far_out, near_out, cls_ref, sem, cls_sem):
    flip = flipped()
    fetch = pltpu.make_async_copy(classes, cls_ref, cls_sem)
    fetch.start()
    loop(lambda r: moved(pops, held, sem, r).start())
    fetch.wait()

    def body(r):
        moved(pops, held, sem, r).wait()
        for p in range(PLANES):
            cls = cls_ref[native(flip, 0, p, r)[1], :]
            om = jnp.full((8, LANES), RATES[0], F32)
            for entry in range(1, 4):
                om = jnp.where(cls == entry, RATES[entry], om)
            om_ref[p, block(r), :] = om
            if p in EDGES:
                i = EDGES.index(p)
                f = get_native(held, flip, p, r)
                rho, u = state_of(f)
                put_velocity(u_ref, u, i, r)
                out = relaxed(f, rho, u, om)
                put_all(post, out, i, r)
                put_crossing(far_out, near_out, out, p, r, 1)

    loop(body)


def first_inner(held, om_ref, post, u_ref):
    flip = flipped()

    def body(r):
        for i, p in enumerate(INNER):
            f = get_native(held, flip, p, r)
            rho, u = state_of(f)
            put_velocity(u_ref, u, i, r)
            put_all(post, relaxed(f, rho, u, om_ref[p, block(r), :]), i, r)

    loop(body)


def cotangent_planes(cot, edge, inner, far_out, near_out):
    flip = flipped()

    def body(r):
        for p in range(PLANES):
            values = get_native(cot, flip, p, r)
            ref, i = plane_of(edge, inner, p)
            put_all(ref, values, i, r)
            if p in EDGES:
                put_crossing(far_out, near_out, values, p, r, -1)

    loop(body)


def forward_inner(edge, inner, om_ref, post, u_ref, ready):
    m = iotas()

    def body(r):
        for i, p in enumerate(INNER):
            f = pull_local(edge, inner, p, r, 1, m)
            rho, u = state_of(f)
            put_velocity(u_ref, u, i, r)
            put_all(post, relaxed(f, rho, u, om_ref[p, block(r), :]), i, r)
        for i, p in enumerate(EDGES):
            put_all(ready, pull_local(edge, inner, p, r, 1, m), i, r)

    loop(body)


def receive(far, near, got, sign, m):
    for r in range(BLOCKS):
        for i, p in enumerate(EDGES):
            for j, k in enumerate(crossing(p, sign)):
                cy, cz = sign * SPEEDS[k][1], sign * SPEEDS[k][2]
                got[j, i, block(r), :] = shifted(far if p == 0 else near, (j,), r, cy, cz, m)


def edge_values(ready, got, i, p, r, sign):
    values = get_some(ready, i, r, crossing(p, sign))
    for j, k in enumerate(crossing(p, sign)):
        values[k] = got[j, i, block(r), :]
    return values


def forward_edges(ready, far, near, om_ref, post, u_ref, far_out, near_out, got):
    receive(far, near, got, 1, iotas())

    def body(r):
        for i, p in enumerate(EDGES):
            f = edge_values(ready, got, i, p, r, 1)
            rho, u = state_of(f)
            put_velocity(u_ref, u, i, r)
            out = relaxed(f, rho, u, om_ref[p, block(r), :])
            put_all(post, out, i, r)
            put_crossing(far_out, near_out, out, p, r, 1)

    loop(body)


def adjoint_inner(edge, inner, om_ref, u_ref, lam, ready):
    m = iotas()

    def body(r):
        for i, p in enumerate(INNER):
            mu = pull_local(edge, inner, p, r, -1, m)
            put_all(lam, adjoint(mu, get_velocity(u_ref, i, r), om_ref[p, block(r), :]), i, r)
        for i, p in enumerate(EDGES):
            put_all(ready, pull_local(edge, inner, p, r, -1, m), i, r)

    loop(body)


def adjoint_top(edge, inner, om_ref, u_ref, far, near, lam, ready):
    m = iotas()

    def body(r):
        for i, p in enumerate(INNER):
            mu = pull_local(edge, inner, p, r, -1, m)
            put_all(lam, adjoint(mu, get_velocity(u_ref, i, r), om_ref[p, block(r), :]), i, r)
        for i, p in enumerate(EDGES):
            mu = pull_local(edge, inner, p, r, -1, m)
            pull_remote(far if p == 0 else near, mu, p, r, -1, m)
            put_all(ready, mu, i, r)

    loop(body)


def adjoint_edges(ready, far, near, om_ref, u_ref, lam, far_out, near_out, got):
    receive(far, near, got, -1, iotas())

    def body(r):
        for i, p in enumerate(EDGES):
            mu = edge_values(ready, got, i, p, r, -1)
            out = adjoint(mu, get_velocity(u_ref, i, r), om_ref[p, block(r), :])
            put_all(lam, out, i, r)
            put_crossing(far_out, near_out, out, p, r, -1)

    loop(body)


def turn_edges(ready, far, near, om_ref, mus, lam, far_out, near_out, got, state):
    receive(far, near, got, 1, iotas())

    def body(r):
        for i, p in enumerate(EDGES):
            rho, u = state_of(edge_values(ready, got, i, p, r, 1))
            put_velocity(state, u + [rho], i, r)
            out = adjoint(get_some(mus, i, r), u, om_ref[p, block(r), :])
            put_all(lam, out, i, r)
            put_crossing(far_out, near_out, out, p, r, -1)

    loop(body)


def relax_edges(ready, got, state, om_ref, post, far_out, near_out):
    def body(r):
        for i, p in enumerate(EDGES):
            f = edge_values(ready, got, i, p, r, 1)
            *u, rho = [state[j, i, block(r), :] for j in range(4)]
            out = relaxed(f, rho, u, om_ref[p, block(r), :])
            put_all(post, out, i, r)
            put_crossing(far_out, near_out, out, p, r, 1)

    loop(body)


def put_mirrored(hold, values, flip, i, r):
    for k in range(19):
        kk = k if MIRROR[k] == k else jnp.where(flip == 1, MIRROR[k], k)
        hold[kk, i, block(r), :] = values[k]


def write_out(hold, result, sem, flip, p, i, r):
    x = jnp.where(flip == 1, PLANES - 1 - p, p)
    return pltpu.make_async_copy(
        hold.at[:, i, block(r), :], result.at[:, block(r), x, :], sem.at[i, r]
    )


def write_all(hold, result, sem, flip, places, each):
    def body(r):
        each(r)
        for i, p in enumerate(places):
            write_out(hold, result, sem, flip, p, i, r).start()

    def wait(r):
        for i, p in enumerate(places):
            write_out(hold, result, sem, flip, p, i, r).wait()

    loop(body)
    loop(wait)


def stream_inner(edge, inner, final, ready, hold, sem):
    flip, m = flipped(), iotas()

    def each(r):
        for i, p in enumerate(INNER):
            put_mirrored(hold, pull_local(edge, inner, p, r, 1, m), flip, i, r)
        for i, p in enumerate(EDGES):
            put_all(ready, pull_local(edge, inner, p, r, 1, m), i, r)

    write_all(hold, final, sem, flip, INNER, each)


def stream_edges(ready, far, near, partial, final, hold, sem, got):
    flip = flipped()
    receive(far, near, got, 1, iotas())

    def each(r):
        for i, p in enumerate(EDGES):
            put_mirrored(hold, edge_values(ready, got, i, p, r, 1), flip, i, r)

    write_all(hold, final, sem, flip, EDGES, each)


def adjoint_inner_last(edge, inner, om_ref, u_ref, grad, ready, hold, sem):
    flip, m = flipped(), iotas()

    def each(r):
        for i, p in enumerate(INNER):
            mu = pull_local(edge, inner, p, r, -1, m)
            out = adjoint(mu, get_velocity(u_ref, i, r), om_ref[p, block(r), :])
            put_mirrored(hold, out, flip, i, r)
        for i, p in enumerate(EDGES):
            put_all(ready, pull_local(edge, inner, p, r, -1, m), i, r)

    write_all(hold, grad, sem, flip, INNER, each)


def adjoint_edges_last(ready, far, near, om_ref, u_ref, partial, grad, hold, sem, got):
    flip = flipped()
    receive(far, near, got, -1, iotas())

    def each(r):
        for i, p in enumerate(EDGES):
            mu = edge_values(ready, got, i, p, r, -1)
            out = adjoint(mu, get_velocity(u_ref, i, r), om_ref[p, block(r), :])
            put_mirrored(hold, out, flip, i, r)

    write_all(hold, grad, sem, flip, EDGES, each)


INSIDE = pl.BlockSpec(memory_space=pltpu.VMEM)
OUTSIDE = pl.BlockSpec(memory_space=pltpu.HBM)
PAIR = (19, 2, ROWS, LANES)
VELOCITY = (3, 2, ROWS, LANES)
RELAX = (PLANES, ROWS, LANES)
CROSS = (5, ROWS, LANES)
NATIVE = (19, PLANES * ROWS, LANES)
SEMS = pltpu.SemaphoreType.DMA((BLOCKS,))
STATE = (4, 2, ROWS, LANES)
CROSSED = (5, 2, ROWS, LANES)
RESULT = (19, ROWS, PLANES, LANES)
STAGED = [pltpu.VMEM(PAIR, F32), pltpu.SemaphoreType.DMA((2, BLOCKS))]
GOT = [pltpu.VMEM(CROSSED, F32)]


def kernel(body, outs, scratch=(), aliases=None):
    def call(*args):
        args = [x if isinstance(x, tuple) else (x, 1) for x in args]
        return pl.pallas_call(
            body,
            in_specs=[INSIDE if inside else OUTSIDE for _, inside in args],
            out_specs=[INSIDE if inside else OUTSIDE for _, inside in outs],
            out_shape=[
                pltpu.VMEM(s, F32) if inside else jax.ShapeDtypeStruct(s, F32) for s, inside in outs
            ],
            scratch_shapes=list(scratch),
            input_output_aliases=aliases or {},
            compiler_params=pltpu.CompilerParams(vmem_limit_bytes=8 * 2**20),
            name=body.__name__,
        )(
            *[
                pltpu.with_memory_space_constraint(x, pltpu.VMEM if inside else pltpu.HBM)
                for x, inside in args
            ]
        )

    return call


def local(populations, relax_class, cotangent):
    count = lax.axis_size("gx")
    near_pairs = [(i, i ^ 1) for i in range(count)]
    far_pairs = [(i, (i + 1 if i % 2 else i - 1) % count) for i in range(count)]

    def exchange(far, near):
        near = lax.ppermute(near, "gx", near_pairs)
        return lax.ppermute(far, "gx", far_pairs), near

    def to_native(x):
        lead = x.shape[:-2]
        x = x.reshape(lead + (PLANES, ROWS, LANES))
        return jnp.swapaxes(x, -3, -2).reshape(lead + (PLANES * ROWS, LANES))

    def from_native(x):
        return jnp.swapaxes(x, 1, 2).reshape(populations.shape)

    pops, classes, cot = to_native(populations), to_native(relax_class), to_native(cotangent)
    pair, speed, cross = (PAIR, 1), (VELOCITY, 1), (CROSS, 1)
    held, om, post_e, u0_e, far, near = kernel(
        first_edges,
        [(NATIVE, 1), (RELAX, 1), pair, speed, cross, cross],
        [pltpu.VMEM(classes.shape, jnp.int32), SEMS, pltpu.SemaphoreType.DMA],
    )((pops, 0), (classes, 0))
    cot, far, near = lax.optimization_barrier((cot, far, near))
    far, near = exchange(far, near)
    post_i, u0_i = kernel(first_inner, [pair, speed])(held, om)
    cot_e, cot_i, farc, nearc = kernel(cotangent_planes, [pair, pair, cross, cross])(cot)
    farc, nearc = exchange(farc, nearc)
    inner = kernel(forward_inner, [pair, speed, pair])

    post_i, u1_i, ready = inner(post_e, post_i, om)
    post_e, u1_e, far, near = kernel(forward_edges, [pair, speed, cross, cross], GOT)(
        ready, far, near, om
    )
    far, near = exchange(far, near)
    post_i, u2_i, ready = inner(post_e, post_i, om)
    lam_i, mus = kernel(adjoint_top, [pair, pair])(cot_e, cot_i, om, u2_i, farc, nearc)
    lam_e, far, near, got, state = kernel(
        turn_edges, [pair, cross, cross, (CROSSED, 1), (STATE, 1)]
    )(ready, far, near, om, mus)
    far, near = exchange(far, near)
    post_e, far_post, near_post = kernel(relax_edges, [pair, cross, cross])(ready, got, state, om)
    far_post, near_post = exchange(far_post, near_post)
    lam_i, ready = kernel(adjoint_inner, [pair, pair])(lam_e, lam_i, om, u1_i)
    final, ready_f = kernel(stream_inner, [(RESULT, 0), pair], STAGED)(post_e, post_i)
    ready, ready_f = lax.optimization_barrier((ready, ready_f))
    lam_e, far, near = kernel(adjoint_edges, [pair, cross, cross], GOT)(ready, far, near, om, u1_e)
    far, near = exchange(far, near)
    grad, ready = kernel(adjoint_inner_last, [(RESULT, 0), pair], STAGED)(lam_e, lam_i, om, u0_i)
    (final,) = kernel(stream_edges, [(RESULT, 0)], STAGED + GOT, {3: 0})(
        ready_f, far_post, near_post, (final, 0)
    )
    (grad,) = kernel(adjoint_edges_last, [(RESULT, 0)], STAGED + GOT, {5: 0})(
        ready, far, near, om, u0_e, (grad, 0)
    )
    return from_native(final), from_native(grad)


def solution(mesh):
    return jax.shard_map(
        local,
        mesh=mesh,
        in_specs=(
            P(None, ("groups", "gx"), None),
            P(("groups", "gx"), None),
            P(None, ("groups", "gx"), None),
        ),
        out_specs=(P(None, ("groups", "gx"), None), P(None, ("groups", "gx"), None)),
        check_vma=False,
    )
```

```python
import jax
import jax.numpy as jnp
from jax import lax
from jax.experimental import pallas as pl
from jax.experimental.pallas import tpu as pltpu
from jax.sharding import PartitionSpec as P

PLANES, ROWS, LANES, BLOCKS = 4, 64, 128, 8
SPEEDS = [
    (0, 0, 0), (1, 0, 0), (-1, 0, 0), (0, 1, 0), (0, -1, 0), (0, 0, 1), (0, 0, -1),
    (1, 1, 0), (-1, -1, 0), (1, -1, 0), (-1, 1, 0), (1, 0, 1), (-1, 0, -1),
    (1, 0, -1), (-1, 0, 1), (0, 1, 1), (0, -1, -1), (0, 1, -1), (0, -1, 1),
]
RATES = [1.0 / 1.0, 1.0 / 1.25, 1.0 / 1.6, 1.0 / 2.4]
MIRROR = [SPEEDS.index((-cx, cy, cz)) for cx, cy, cz in SPEEDS]
PLUS = [k for k in range(19) if SPEEDS[k][0] == 1]
MINUS = [MIRROR[k] for k in PLUS]
F32 = jnp.float32


def iotas():
    lane = lax.broadcasted_iota(jnp.int32, (8, LANES), 1)
    row = lax.broadcasted_iota(jnp.int32, (8, LANES), 0)
    turns = {}
    for turn in (0, 64):
        for cz in (1, -1):
            turns[turn, cz] = ((lane & 64) ^ turn) | ((lane - cz) & 63)
    return {"high": lane >= 64, "top": row == 0, "bottom": row == 7, **turns}


def block(r):
    return pl.ds(r * 8 if isinstance(r, int) else pl.multiple_of(r * 8, 8), 8)


def shifted(ref, index, r, cy, cz, m):
    here = ref[index + (block(r), slice(None))]
    turn = 0
    if cy == 1:
        edge = ref[index + (pl.ds(((r + 7) & 7) * 8 + 7, 1), slice(None))]
        other = jnp.where(m["top"], edge, pltpu.roll(here, 1, 0))
        here, turn = jnp.where(m["high"], other, here), 64
    elif cy == -1:
        edge = ref[index + (pl.ds(((r + 1) & 7) * 8, 1), slice(None))]
        other = jnp.where(m["bottom"], edge, pltpu.roll(here, 7, 0))
        here, turn = jnp.where(m["high"], here, other), 64
    if cz == 0:
        return pltpu.roll(here, turn, 1) if turn else here
    return jnp.take_along_axis(here, m[turn, cz], axis=1)


def moments(f):
    s = [f[k] + f[k + 1] for k in range(1, 19, 2)]
    d = [f[k] - f[k + 1] for k in range(1, 19, 2)]
    rho = f[0] + ((s[0] + s[1]) + (s[2] + s[3])) + ((s[4] + s[5]) + (s[6] + s[7])) + s[8]
    jx = d[0] + ((d[3] + d[4]) + (d[5] + d[6]))
    jy = d[1] + ((d[3] - d[4]) + (d[7] + d[8]))
    jz = d[2] + ((d[5] - d[6]) + (d[7] - d[8]))
    return rho, jx, jy, jz


def along_odd(k, v):
    total = None
    for c, x in zip(SPEEDS[k], v):
        if c:
            total = x if total is None else (total + x if c == 1 else total - x)
    return total


def relaxed(f, rho, u, om):
    keep = 1.0 - om
    wr = om * rho
    shape = 1.0 - 1.5 * (u[0] * u[0] + u[1] * u[1] + u[2] * u[2])
    out = [None] * 19
    out[0] = keep * f[0] + (wr * (1.0 / 3.0)) * shape
    for first, last, w in ((1, 7, 1.0 / 18.0), (7, 19, 1.0 / 36.0)):
        part = wr * w
        base, lin, quad = part * shape, part * 3.0, part * 4.5
        for k in range(first, last, 2):
            a = along_odd(k, u)
            even, odd = base + quad * (a * a), lin * a
            out[k] = keep * f[k] + (even + odd)
            out[k + 1] = keep * f[k + 1] + (even - odd)
    return out


def adjoint(mu, u, om):
    s = [None] + [mu[k] + mu[k + 1] for k in range(1, 19, 2)]
    d = [None] + [mu[k] - mu[k + 1] for k in range(1, 19, 2)]
    a, b = 1.0 / 18.0, 1.0 / 36.0
    s45, s67, s89 = s[4] + s[5], s[6] + s[7], s[8] + s[9]
    xx = a * s[1] + b * (s45 + s67)
    yy = a * s[2] + b * (s45 + s89)
    zz = a * s[3] + b * (s67 + s89)
    m0 = (1.0 / 3.0) * mu[0] + a * ((s[1] + s[2]) + s[3]) + b * ((s45 + s67) + s89)
    xy, xz, yz = b * (s[4] - s[5]), b * (s[6] - s[7]), b * (s[8] - s[9])
    mx = a * d[1] + b * ((d[4] + d[5]) + (d[6] + d[7]))
    my = a * d[2] + b * ((d[4] - d[5]) + (d[8] + d[9]))
    mz = a * d[3] + b * ((d[6] - d[7]) + (d[8] - d[9]))
    vx = xx * u[0] + xy * u[1] + xz * u[2]
    vy = xy * u[0] + yy * u[1] + yz * u[2]
    vz = xz * u[0] + yz * u[1] + zz * u[2]
    uu = u[0] * u[0] + u[1] * u[1] + u[2] * u[2]
    rho_part = om * (m0 + 1.5 * (m0 * uu) - 4.5 * (u[0] * vx + u[1] * vy + u[2] * vz))
    om3 = 3.0 * om
    flow = [
        om3 * (mx + 3.0 * vx - u[0] * m0),
        om3 * (my + 3.0 * vy - u[1] * m0),
        om3 * (mz + 3.0 * vz - u[2] * m0),
    ]
    keep = 1.0 - om
    out = [None] * 19
    out[0] = keep * mu[0] + rho_part
    for k in range(1, 19, 2):
        g = along_odd(k, flow)
        out[k] = keep * mu[k] + (rho_part + g)
        out[k + 1] = keep * mu[k + 1] + (rho_part - g)
    return out


FAR, NEAR, INNER = 0, PLANES - 1, (1, 2)


def plane_of(parts, p):
    far, inner, near = parts
    return (far, ()) if p == FAR else (near, ()) if p == NEAR else (inner, (INNER.index(p),))


def pull_local(parts, p, r, sign, m):
    out = [None] * 19
    for k in range(19):
        cx, cy, cz = (sign * c for c in SPEEDS[k])
        if 0 <= p - cx < PLANES:
            ref, i = plane_of(parts, p - cx)
            out[k] = shifted(ref, (k,) + i, r, cy, cz, m)
    return out


def crossing(p, sign):
    return (PLUS, MINUS)[(sign == 1) != (p == FAR)]


def pull_remote(other, out, p, r, sign, m):
    for i, k in enumerate(crossing(p, sign)):
        out[k] = shifted(other, (i,), r, sign * SPEEDS[k][1], sign * SPEEDS[k][2], m)
    return out


def put(ref, values, r, i=()):
    for k, value in enumerate(values):
        if value is not None:
            ref[(k,) + i + (block(r), slice(None))] = value


def get(ref, r, i=(), count=19, missing=()):
    return [
        None if k in missing else ref[(k,) + i + (block(r), slice(None))] for k in range(count)
    ]


def put_crossing(ref, values, p, r, sign):
    put(ref, [values[k] for k in crossing(p, -sign)], r)


def state_of(f):
    rho, jx, jy, jz = moments(f)
    inv = 1.0 / rho
    return rho, [jx * inv, jy * inv, jz * inv]


def native(flip, k, p, r):
    kk = k if MIRROR[k] == k else jnp.where(flip == 1, MIRROR[k], k)
    x = jnp.where(flip == 1, PLANES - 1 - p, p)
    return kk, pl.ds(r * (8 * PLANES) + x, 8, stride=PLANES)


def get_native(ref, flip, p, r):
    out = []
    for k in range(19):
        kk, rows = native(flip, k, p, r)
        out.append(ref[kk, rows, :])
    return out


def put_native(ref, values, flip, p, r):
    for k in range(19):
        kk, rows = native(flip, k, p, r)
        ref[kk, rows, :] = values[k]


def put_mirrored(hold, values, flip, r, i=()):
    for k in range(19):
        kk = k if MIRROR[k] == k else jnp.where(flip == 1, MIRROR[k], k)
        hold[(kk,) + i + (block(r), slice(None))] = values[k]


def loop(body, step=1):
    def steps(r, carry):
        for j in range(step):
            body(r * step + j)
        return carry

    lax.fori_loop(0, BLOCKS // step, steps, 0)


def chunk(ref, r):
    rows = 8 * PLANES
    return ref.at[:, pl.ds(pl.multiple_of(r * rows, rows), rows), :]


def moved(source, target, sem, r):
    return pltpu.make_async_copy(chunk(source, r), chunk(target, r), sem.at[r])


def write_out(hold, result, sem, flip, p, r):
    x = jnp.where(flip == 1, PLANES - 1 - p, p)
    return pltpu.make_async_copy(hold.at[:, block(r), :], result.at[:, block(r), x, :], sem.at[r])


def flipped():
    return lax.rem(lax.axis_index("gx"), 2)


def first_edges(
    pops, classes, held, om_ref, post_f, post_n, u_f, u_n, far_out, near_out, cls_ref, sem, cls_sem
):
    flip = flipped()
    fetch = pltpu.make_async_copy(classes, cls_ref, cls_sem)
    fetch.start()
    loop(lambda r: moved(pops, held, sem, r).start())
    fetch.wait()

    def body(r):
        moved(pops, held, sem, r).wait()
        for p in range(PLANES):
            cls = cls_ref[native(flip, 0, p, r)[1], :]
            om = jnp.full((8, LANES), RATES[0], F32)
            for entry in range(1, 4):
                om = jnp.where(cls == entry, RATES[entry], om)
            om_ref[p, block(r), :] = om
            if p in INNER:
                continue
            f = get_native(held, flip, p, r)
            rho, u = state_of(f)
            put(u_f if p == FAR else u_n, u, r)
            out = relaxed(f, rho, u, om)
            put(post_f if p == FAR else post_n, out, r)
            put_crossing(far_out if p == FAR else near_out, out, p, r, 1)

    loop(body)


def first_inner(held, om_ref, post, u_ref):
    flip = flipped()

    def body(r):
        for i, p in enumerate(INNER):
            f = get_native(held, flip, p, r)
            rho, u = state_of(f)
            put(u_ref, u, r, (i,))
            put(post, relaxed(f, rho, u, om_ref[p, block(r), :]), r, (i,))

    loop(body)


def cotangent_planes(cot, far, inner, near, far_out, near_out):
    flip = flipped()

    def body(r):
        for p in range(PLANES):
            values = get_native(cot, flip, p, r)
            ref, i = plane_of((far, inner, near), p)
            put(ref, values, r, i)
            if p not in INNER:
                put_crossing(far_out if p == FAR else near_out, values, p, r, -1)

    loop(body)


def forward_inner(far, inner, near, om_ref, post, u_ref, ready_f, ready_n):
    parts, m = (far, inner, near), iotas()

    def body(r):
        for i, p in enumerate(INNER):
            f = pull_local(parts, p, r, 1, m)
            rho, u = state_of(f)
            put(u_ref, u, r, (i,))
            put(post, relaxed(f, rho, u, om_ref[p, block(r), :]), r, (i,))
        for p, ready in ((FAR, ready_f), (NEAR, ready_n)):
            put(ready, pull_local(parts, p, r, 1, m), r)

    loop(body, STEP)


def receive(other, got, p, sign):
    m = iotas()
    for r in range(BLOCKS):
        for j, k in enumerate(crossing(p, sign)):
            cy, cz = sign * SPEEDS[k][1], sign * SPEEDS[k][2]
            got[j, block(r), :] = shifted(other, (j,), r, cy, cz, m)


def edge_values(ready, got, p, r, sign):
    values = get(ready, r, missing=crossing(p, sign))
    for j, k in enumerate(crossing(p, sign)):
        values[k] = got[j, block(r), :]
    return values


def forward_edge(p):
    def forward_edge(ready, other, om_ref, post, u_ref, out_ref, got):
        receive(other, got, p, 1)

        def body(r):
            f = edge_values(ready, got, p, r, 1)
            rho, u = state_of(f)
            put(u_ref, u, r)
            out = relaxed(f, rho, u, om_ref[p, block(r), :])
            put(post, out, r)
            put_crossing(out_ref, out, p, r, 1)

        loop(body, 2)

    return forward_edge


def adjoint_planes(parts, om_ref, u_ref, lam, r, m):
    for i, p in enumerate(INNER):
        mu = pull_local(parts, p, r, -1, m)
        out = adjoint(mu, get(u_ref, r, (i,), 3), om_ref[p, block(r), :])
        put(lam, out, r, (i,))


def adjoint_inner(far, inner, near, om_ref, u_ref, lam, ready_f, ready_n):
    parts, m = (far, inner, near), iotas()

    def body(r):
        adjoint_planes(parts, om_ref, u_ref, lam, r, m)
        for p, ready in ((FAR, ready_f), (NEAR, ready_n)):
            put(ready, pull_local(parts, p, r, -1, m), r)

    loop(body, STEP)


def adjoint_top(far, inner, near, om_ref, u_ref, other_f, other_n, lam, mus_f, mus_n):
    parts, m = (far, inner, near), iotas()

    def body(r):
        adjoint_planes(parts, om_ref, u_ref, lam, r, m)
        for p, mus, other in ((FAR, mus_f, other_f), (NEAR, mus_n, other_n)):
            put(mus, pull_remote(other, pull_local(parts, p, r, -1, m), p, r, -1, m), r)

    loop(body, STEP)


def adjoint_edge(p):
    def adjoint_edge(ready, other, om_ref, u_ref, lam, out_ref, got):
        receive(other, got, p, -1)

        def body(r):
            mu = edge_values(ready, got, p, r, -1)
            out = adjoint(mu, get(u_ref, r, count=3), om_ref[p, block(r), :])
            put(lam, out, r)
            put_crossing(out_ref, out, p, r, -1)

        loop(body, 2)

    return adjoint_edge


def turn_edge(p):
    def turn_edge(ready, other, om_ref, mus, lam, out_ref, got, state):
        receive(other, got, p, 1)

        def body(r):
            rho, u = state_of(edge_values(ready, got, p, r, 1))
            put(state, u + [rho], r)
            out = adjoint(get(mus, r), u, om_ref[p, block(r), :])
            put(lam, out, r)
            put_crossing(out_ref, out, p, r, -1)

        loop(body, 2)

    return turn_edge


def relax_edges(ready_f, got_f, state_f, ready_n, got_n, state_n, om_ref, post_f, post_n, out_f, out_n):
    def body(r):
        for p, ready, got, state, post, out_ref in (
            (FAR, ready_f, got_f, state_f, post_f, out_f),
            (NEAR, ready_n, got_n, state_n, post_n, out_n),
        ):
            f = edge_values(ready, got, p, r, 1)
            *u, rho = get(state, r, count=4)
            out = relaxed(f, rho, u, om_ref[p, block(r), :])
            put(post, out, r)
            put_crossing(out_ref, out, p, r, 1)

    loop(body)


def finish(
    far, inner, near, om_ref, u_ref, post_f, post_i, post_n, other_f, other_n,
    grad, ready_f, ready_n, final, hold_1, hold_2, hold, sem_1, sem_2, sem,
):
    flip, parts, m = flipped(), (far, inner, near), iotas()
    posts, places = (post_f, post_i, post_n), ((1, hold_1, sem_1), (2, hold_2, sem_2))

    def body(r):
        for i, (p, keep, done) in enumerate(places):
            mu = pull_local(parts, p, r, -1, m)
            out = adjoint(mu, get(u_ref, r, (i,), 3), om_ref[p, block(r), :])
            put_mirrored(keep, out, flip, r)
            write_out(keep, grad, done, flip, p, r).start()
        for p, ready in ((FAR, ready_f), (NEAR, ready_n)):
            put(ready, pull_local(parts, p, r, -1, m), r)

    def stream(r):
        for p in range(PLANES):
            f = pull_local(posts, p, r, 1, m)
            if p not in INNER:
                pull_remote(other_f if p == FAR else other_n, f, p, r, 1, m)
            put_native(hold, f, flip, p, r)
        moved(hold, final, sem, r).start()

    def wait(r):
        for p, keep, done in places:
            write_out(keep, grad, done, flip, p, r).wait()
        moved(hold, final, sem, r).wait()

    loop(body, STEP)
    loop(stream, STEP)
    loop(wait)


def adjoint_edge_last(p):
    def adjoint_edge_last(ready, other, om_ref, u_ref, partial, grad, hold, sem, got):
        flip = flipped()
        receive(other, got, p, -1)

        def body(r):
            mu = edge_values(ready, got, p, r, -1)
            out = adjoint(mu, get(u_ref, r, count=3), om_ref[p, block(r), :])
            put_mirrored(hold, out, flip, r)

        def both(r):
            for j in range(2):
                body(2 * r + j)
            for j in range(2):
                write_out(hold, grad, sem, flip, p, 2 * r + j).start()

        lax.fori_loop(0, BLOCKS // 2, lambda r, c: (both(r), c)[1], 0)
        loop(lambda r: write_out(hold, grad, sem, flip, p, r).wait())

    return adjoint_edge_last


INSIDE = pl.BlockSpec(memory_space=pltpu.VMEM)
OUTSIDE = pl.BlockSpec(memory_space=pltpu.HBM)
STEP = 2
INNERS = (19, 2, ROWS, LANES)
PLANE = (19, ROWS, LANES)
RELAX = (PLANES, ROWS, LANES)
CROSS = (5, ROWS, LANES)
NATIVE = (19, PLANES * ROWS, LANES)
RESULT = (19, ROWS, PLANES, LANES)
SEMS = pltpu.SemaphoreType.DMA((BLOCKS,))
GOT = [pltpu.VMEM(CROSS, F32)]


def kernel(body, outs, scratch=(), aliases=None):
    def call(*args):
        args = [x if isinstance(x, tuple) else (x, 1) for x in args]
        return pl.pallas_call(
            body,
            in_specs=[INSIDE if inside else OUTSIDE for _, inside in args],
            out_specs=[INSIDE if inside else OUTSIDE for _, inside in outs],
            out_shape=[
                pltpu.VMEM(s, F32) if inside else jax.ShapeDtypeStruct(s, F32) for s, inside in outs
            ],
            scratch_shapes=list(scratch),
            input_output_aliases=aliases or {},
            compiler_params=pltpu.CompilerParams(vmem_limit_bytes=8 * 2**20),
            name=body.__name__,
        )(
            *[
                pltpu.with_memory_space_constraint(x, pltpu.VMEM if inside else pltpu.HBM)
                for x, inside in args
            ]
        )

    return call


def local(populations, relax_class, cotangent):
    count = lax.axis_size("gx")
    near_pairs = [(i, i ^ 1) for i in range(count)]
    far_pairs = [(i, (i + 1 if i % 2 else i - 1) % count) for i in range(count)]

    def exchange(far, near):
        near = lax.ppermute(near, "gx", near_pairs)
        return lax.ppermute(far, "gx", far_pairs), near

    def to_native(x):
        lead = x.shape[:-2]
        x = x.reshape(lead + (PLANES, ROWS, LANES))
        return jnp.swapaxes(x, -3, -2).reshape(lead + (PLANES * ROWS, LANES))

    pops, classes, cot = to_native(populations), to_native(relax_class), to_native(cotangent)
    inners, plane, cross = (INNERS, 1), (PLANE, 1), (CROSS, 1)
    speed, speeds, state = ((3, ROWS, LANES), 1), ((3, 2, ROWS, LANES), 1), ((4, ROWS, LANES), 1)
    held, om, post_f, post_n, u0_f, u0_n, far, near = kernel(
        first_edges,
        [(NATIVE, 1), (RELAX, 1), plane, plane, speed, speed, cross, cross],
        [pltpu.VMEM(classes.shape, jnp.int32), SEMS, pltpu.SemaphoreType.DMA],
    )((pops, 0), (classes, 0))
    far, near = exchange(far, near)
    post_i, u0_i = kernel(first_inner, [inners, speeds])(held, om)
    cot_f, cot_i, cot_n, cfar, cnear = kernel(cotangent_planes, [plane, inners, plane, cross, cross])(
        cot
    )
    cfar, cnear = exchange(cfar, cnear)
    inner = kernel(forward_inner, [inners, speeds, plane, plane])
    edge = [kernel(forward_edge(p), [plane, speed, cross], GOT) for p in (FAR, NEAR)]

    post_i, u1_i, ready_f, ready_n = inner(post_f, post_i, post_n, om)
    post_n, u1_n, near = edge[1](ready_n, near, om)
    post_f, u1_f, far = edge[0](ready_f, far, om)
    far, near = exchange(far, near)
    post_i, u2_i, ready_f, ready_n = inner(post_f, post_i, post_n, om)
    lam_i, mus_f, mus_n = kernel(adjoint_top, [inners, plane, plane])(
        cot_f, cot_i, cot_n, om, u2_i, cfar, cnear
    )
    turn = [kernel(turn_edge(p), [plane, cross, cross, state]) for p in (FAR, NEAR)]
    lam_n, near, got_n, state_n = turn[1](ready_n, near, om, mus_n)
    lam_f, far, got_f, state_f = turn[0](ready_f, far, om, mus_f)
    far, near = exchange(far, near)
    post_f, post_n, pfar, pnear = kernel(relax_edges, [plane, plane, cross, cross])(
        ready_f, got_f, state_f, ready_n, got_n, state_n, om
    )
    lam_i, ready_f, ready_n = kernel(adjoint_inner, [inners, plane, plane])(
        lam_f, lam_i, lam_n, om, u1_i
    )
    pfar, pnear, ready_f = lax.optimization_barrier((pfar, pnear, ready_f))
    pfar, pnear = exchange(pfar, pnear)
    edge = [kernel(adjoint_edge(p), [plane, cross], GOT) for p in (FAR, NEAR)]
    lam_n, near = edge[1](ready_n, near, om, u1_n)
    lam_f, far = edge[0](ready_f, far, om, u1_f)
    far, near = exchange(far, near)
    holds = [pltpu.VMEM(PLANE, F32), pltpu.VMEM(PLANE, F32), pltpu.VMEM(NATIVE, F32), SEMS, SEMS, SEMS]
    grad, ready_f, ready_n, final = kernel(finish, [(RESULT, 0), plane, plane, (NATIVE, 0)], holds)(
        lam_f, lam_i, lam_n, om, u0_i, post_f, post_i, post_n, pfar, pnear
    )
    scratch = [pltpu.VMEM(PLANE, F32), SEMS] + GOT
    last = [kernel(adjoint_edge_last(p), [(RESULT, 0)], scratch, {4: 0}) for p in (FAR, NEAR)]
    (grad,) = last[1](ready_n, near, om, u0_n, (grad, 0))
    (grad,) = last[0](ready_f, far, om, u0_f, (grad, 0))
    final = jnp.swapaxes(final.reshape(19, ROWS, PLANES, LANES), 1, 2)
    return final.reshape(populations.shape), jnp.swapaxes(grad, 1, 2).reshape(populations.shape)


def solution(mesh):
    return jax.shard_map(
        local,
        mesh=mesh,
        in_specs=(
            P(None, ("groups", "gx"), None),
            P(("groups", "gx"), None),
            P(None, ("groups", "gx"), None),
        ),
        out_specs=(P(None, ("groups", "gx"), None), P(None, ("groups", "gx"), None)),
        check_vma=False,
    )
```

```python
import jax
import jax.numpy as jnp
from jax import lax
from jax.experimental import pallas as pl
from jax.experimental.pallas import tpu as pltpu
from jax.sharding import PartitionSpec as P

PLANES, ROWS, LANES, BLOCKS = 4, 64, 128, 8
SPEEDS = [
    (0, 0, 0), (1, 0, 0), (-1, 0, 0), (0, 1, 0), (0, -1, 0), (0, 0, 1), (0, 0, -1),
    (1, 1, 0), (-1, -1, 0), (1, -1, 0), (-1, 1, 0), (1, 0, 1), (-1, 0, -1),
    (1, 0, -1), (-1, 0, 1), (0, 1, 1), (0, -1, -1), (0, 1, -1), (0, -1, 1),
]
RATES = [1.0 / 1.0, 1.0 / 1.25, 1.0 / 1.6, 1.0 / 2.4]
MIRROR = [SPEEDS.index((-cx, cy, cz)) for cx, cy, cz in SPEEDS]
PLUS = [k for k in range(19) if SPEEDS[k][0] == 1]
MINUS = [MIRROR[k] for k in PLUS]
F32 = jnp.float32


def iotas():
    lane = lax.broadcasted_iota(jnp.int32, (8, LANES), 1)
    row = lax.broadcasted_iota(jnp.int32, (8, LANES), 0)
    turns = {}
    for turn in (0, 64):
        for cz in (1, -1):
            turns[turn, cz] = ((lane & 64) ^ turn) | ((lane - cz) & 63)
    return {"high": lane >= 64, "top": row == 0, "bottom": row == 7, **turns}


def block(r):
    return pl.ds(r * 8 if isinstance(r, int) else pl.multiple_of(r * 8, 8), 8)


def shifted(ref, index, r, cy, cz, m):
    here = ref[index + (block(r), slice(None))]
    turn = 0
    if cy == 1:
        edge = ref[index + (pl.ds(((r + 7) & 7) * 8 + 7, 1), slice(None))]
        other = jnp.where(m["top"], edge, pltpu.roll(here, 1, 0))
        here, turn = jnp.where(m["high"], other, here), 64
    elif cy == -1:
        edge = ref[index + (pl.ds(((r + 1) & 7) * 8, 1), slice(None))]
        other = jnp.where(m["bottom"], edge, pltpu.roll(here, 7, 0))
        here, turn = jnp.where(m["high"], here, other), 64
    if cz == 0:
        return pltpu.roll(here, turn, 1) if turn else here
    return jnp.take_along_axis(here, m[turn, cz], axis=1)


def moments(f):
    s = [f[k] + f[k + 1] for k in range(1, 19, 2)]
    d = [f[k] - f[k + 1] for k in range(1, 19, 2)]
    rho = f[0] + ((s[0] + s[1]) + (s[2] + s[3])) + ((s[4] + s[5]) + (s[6] + s[7])) + s[8]
    jx = d[0] + ((d[3] + d[4]) + (d[5] + d[6]))
    jy = d[1] + ((d[3] - d[4]) + (d[7] + d[8]))
    jz = d[2] + ((d[5] - d[6]) + (d[7] - d[8]))
    return rho, jx, jy, jz


def along_odd(k, v):
    total = None
    for c, x in zip(SPEEDS[k], v):
        if c:
            total = x if total is None else (total + x if c == 1 else total - x)
    return total


def relaxed(f, rho, u, om):
    keep = 1.0 - om
    wr = om * rho
    shape = 1.0 - 1.5 * (u[0] * u[0] + u[1] * u[1] + u[2] * u[2])
    out = [None] * 19
    out[0] = keep * f[0] + (wr * (1.0 / 3.0)) * shape
    for first, last, w in ((1, 7, 1.0 / 18.0), (7, 19, 1.0 / 36.0)):
        part = wr * w
        base, lin, quad = part * shape, part * 3.0, part * 4.5
        for k in range(first, last, 2):
            a = along_odd(k, u)
            even, odd = base + quad * (a * a), lin * a
            out[k] = keep * f[k] + (even + odd)
            out[k + 1] = keep * f[k + 1] + (even - odd)
    return out


def adjoint(mu, u, om):
    s = [None] + [mu[k] + mu[k + 1] for k in range(1, 19, 2)]
    d = [None] + [mu[k] - mu[k + 1] for k in range(1, 19, 2)]
    a, b = 1.0 / 18.0, 1.0 / 36.0
    s45, s67, s89 = s[4] + s[5], s[6] + s[7], s[8] + s[9]
    xx = a * s[1] + b * (s45 + s67)
    yy = a * s[2] + b * (s45 + s89)
    zz = a * s[3] + b * (s67 + s89)
    m0 = (1.0 / 3.0) * mu[0] + a * ((s[1] + s[2]) + s[3]) + b * ((s45 + s67) + s89)
    xy, xz, yz = b * (s[4] - s[5]), b * (s[6] - s[7]), b * (s[8] - s[9])
    mx = a * d[1] + b * ((d[4] + d[5]) + (d[6] + d[7]))
    my = a * d[2] + b * ((d[4] - d[5]) + (d[8] + d[9]))
    mz = a * d[3] + b * ((d[6] - d[7]) + (d[8] - d[9]))
    vx = xx * u[0] + xy * u[1] + xz * u[2]
    vy = xy * u[0] + yy * u[1] + yz * u[2]
    vz = xz * u[0] + yz * u[1] + zz * u[2]
    uu = u[0] * u[0] + u[1] * u[1] + u[2] * u[2]
    rho_part = om * (m0 + 1.5 * (m0 * uu) - 4.5 * (u[0] * vx + u[1] * vy + u[2] * vz))
    om3 = 3.0 * om
    flow = [
        om3 * (mx + 3.0 * vx - u[0] * m0),
        om3 * (my + 3.0 * vy - u[1] * m0),
        om3 * (mz + 3.0 * vz - u[2] * m0),
    ]
    keep = 1.0 - om
    out = [None] * 19
    out[0] = keep * mu[0] + rho_part
    for k in range(1, 19, 2):
        g = along_odd(k, flow)
        out[k] = keep * mu[k] + (rho_part + g)
        out[k + 1] = keep * mu[k + 1] + (rho_part - g)
    return out


FAR, NEAR, INNER = 0, PLANES - 1, (1, 2)


def plane_of(parts, p):
    far, inner, near = parts
    return (far, ()) if p == FAR else (near, ()) if p == NEAR else (inner, (INNER.index(p),))


def pull_local(parts, p, r, sign, m):
    out = [None] * 19
    for k in range(19):
        cx, cy, cz = (sign * c for c in SPEEDS[k])
        if 0 <= p - cx < PLANES:
            ref, i = plane_of(parts, p - cx)
            out[k] = shifted(ref, (k,) + i, r, cy, cz, m)
    return out


def crossing(p, sign):
    return (PLUS, MINUS)[(sign == 1) != (p == FAR)]


def pull_remote(other, out, p, r, sign, m):
    for i, k in enumerate(crossing(p, sign)):
        out[k] = shifted(other, (i,), r, sign * SPEEDS[k][1], sign * SPEEDS[k][2], m)
    return out


def put(ref, values, r, i=()):
    for k, value in enumerate(values):
        if value is not None:
            ref[(k,) + i + (block(r), slice(None))] = value


def get(ref, r, i=(), count=19, missing=()):
    return [
        None if k in missing else ref[(k,) + i + (block(r), slice(None))] for k in range(count)
    ]


def put_crossing(ref, values, p, r, sign):
    put(ref, [values[k] for k in crossing(p, -sign)], r)


def state_of(f):
    rho, jx, jy, jz = moments(f)
    inv = 1.0 / rho
    return rho, [jx * inv, jy * inv, jz * inv]


def by_side(run):
    side = lax.rem(lax.axis_index("gx"), 2)
    for flip in (0, 1):
        pl.when(side == flip)(lambda flip=flip: run(flip))


def native(flip, k, p, r):
    return mirrored(flip, k), pl.ds(r * (8 * PLANES) + place(flip, p), 8, stride=PLANES)


def mirrored(flip, k):
    return MIRROR[k] if flip else k


def place(flip, p):
    return PLANES - 1 - p if flip else p


def get_native(ref, flip, p, r):
    out = []
    for k in range(19):
        kk, rows = native(flip, k, p, r)
        out.append(ref[kk, rows, :])
    return out


def put_native(ref, values, flip, p, r):
    for k in range(19):
        kk, rows = native(flip, k, p, r)
        ref[kk, rows, :] = values[k]


def put_mirrored(hold, values, flip, r, i=()):
    for k in range(19):
        hold[(mirrored(flip, k),) + i + (block(r), slice(None))] = values[k]


def loop(body, step=1):
    def steps(r, carry):
        for j in range(step):
            body(r * step + j)
        return carry

    lax.fori_loop(0, BLOCKS // step, steps, 0)


def chunk(ref, r):
    rows = 8 * PLANES
    return ref.at[:, pl.ds(pl.multiple_of(r * rows, rows), rows), :]


def moved(source, target, sem, r):
    return pltpu.make_async_copy(chunk(source, r), chunk(target, r), sem.at[r])


def first_edges(
    pops, classes, held, om_ref, post_f, post_n, u_f, u_n, far_out, near_out, cls_ref, sem, cls_sem
):
    fetch = pltpu.make_async_copy(classes, cls_ref, cls_sem)
    fetch.start()
    loop(lambda r: moved(pops, held, sem, r).start())
    fetch.wait()

    def run(flip):
        def body(r):
            moved(pops, held, sem, r).wait()
            for p in range(PLANES):
                cls = cls_ref[native(flip, 0, p, r)[1], :]
                om = jnp.full((8, LANES), RATES[0], F32)
                for entry in range(1, 4):
                    om = jnp.where(cls == entry, RATES[entry], om)
                om_ref[p, block(r), :] = om
                if p in INNER:
                    continue
                f = get_native(held, flip, p, r)
                rho, u = state_of(f)
                put(u_f if p == FAR else u_n, u, r)
                out = relaxed(f, rho, u, om)
                put(post_f if p == FAR else post_n, out, r)
                put_crossing(far_out if p == FAR else near_out, out, p, r, 1)

        loop(body)

    by_side(run)


def first_inner(held, om_ref, post, u_ref):
    def run(flip):
        def body(r):
            for i, p in enumerate(INNER):
                f = get_native(held, flip, p, r)
                rho, u = state_of(f)
                put(u_ref, u, r, (i,))
                put(post, relaxed(f, rho, u, om_ref[p, block(r), :]), r, (i,))

        loop(body)

    by_side(run)


def cotangent_planes(cot, far, inner, near, far_out, near_out):
    def run(flip):
        def body(r):
            for p in range(PLANES):
                values = get_native(cot, flip, p, r)
                ref, i = plane_of((far, inner, near), p)
                put(ref, values, r, i)
                if p not in INNER:
                    put_crossing(far_out if p == FAR else near_out, values, p, r, -1)

        loop(body)

    by_side(run)


def forward_inner(far, inner, near, om_ref, post, u_ref, ready_f, ready_n):
    parts, m = (far, inner, near), iotas()

    def body(r):
        for i, p in enumerate(INNER):
            f = pull_local(parts, p, r, 1, m)
            rho, u = state_of(f)
            put(u_ref, u, r, (i,))
            put(post, relaxed(f, rho, u, om_ref[p, block(r), :]), r, (i,))
        for p, ready in ((FAR, ready_f), (NEAR, ready_n)):
            put(ready, pull_local(parts, p, r, 1, m), r)

    loop(body, STEP)


def receive(other, got, p, sign):
    m = iotas()
    for r in range(BLOCKS):
        for j, k in enumerate(crossing(p, sign)):
            cy, cz = sign * SPEEDS[k][1], sign * SPEEDS[k][2]
            got[j, block(r), :] = shifted(other, (j,), r, cy, cz, m)


def edge_values(ready, got, p, r, sign):
    values = get(ready, r, missing=crossing(p, sign))
    for j, k in enumerate(crossing(p, sign)):
        values[k] = got[j, block(r), :]
    return values


def forward_edges(
    ready_f, ready_n, far, near, om_ref,
    post_f, post_n, u_f, u_n, out_f, out_n, got_f, got_n,
):
    sides = (
        (FAR, ready_f, far, post_f, u_f, out_f, got_f),
        (NEAR, ready_n, near, post_n, u_n, out_n, got_n),
    )
    for p, _, other, _, _, _, got in sides:
        receive(other, got, p, 1)

    def body(r):
        for p, ready, _, post, u_ref, out_ref, got in sides:
            f = edge_values(ready, got, p, r, 1)
            rho, u = state_of(f)
            put(u_ref, u, r)
            out = relaxed(f, rho, u, om_ref[p, block(r), :])
            put(post, out, r)
            put_crossing(out_ref, out, p, r, 1)

    loop(body)


def adjoint_planes(parts, om_ref, u_ref, lam, r, m):
    for i, p in enumerate(INNER):
        mu = pull_local(parts, p, r, -1, m)
        out = adjoint(mu, get(u_ref, r, (i,), 3), om_ref[p, block(r), :])
        put(lam, out, r, (i,))


def adjoint_inner(far, inner, near, om_ref, u_ref, lam, ready_f, ready_n):
    parts, m = (far, inner, near), iotas()

    def body(r):
        adjoint_planes(parts, om_ref, u_ref, lam, r, m)
        for p, ready in ((FAR, ready_f), (NEAR, ready_n)):
            put(ready, pull_local(parts, p, r, -1, m), r)

    loop(body, STEP)


def adjoint_top(far, inner, near, om_ref, u_ref, other_f, other_n, lam, mus_f, mus_n):
    parts, m = (far, inner, near), iotas()

    def body(r):
        adjoint_planes(parts, om_ref, u_ref, lam, r, m)
        for p, mus, other in ((FAR, mus_f, other_f), (NEAR, mus_n, other_n)):
            put(mus, pull_remote(other, pull_local(parts, p, r, -1, m), p, r, -1, m), r)

    loop(body, STEP)


def adjoint_edge(p):
    def adjoint_edge(ready, other, om_ref, u_ref, lam, out_ref, got):
        receive(other, got, p, -1)

        def body(r):
            mu = edge_values(ready, got, p, r, -1)
            out = adjoint(mu, get(u_ref, r, count=3), om_ref[p, block(r), :])
            put(lam, out, r)
            put_crossing(out_ref, out, p, r, -1)

        loop(body, 2)

    return adjoint_edge


def turn_edge(p):
    def turn_edge(ready, other, om_ref, mus, lam, out_ref, got, state):
        receive(other, got, p, 1)

        def body(r):
            rho, u = state_of(edge_values(ready, got, p, r, 1))
            put(state, u + [rho], r)
            out = adjoint(get(mus, r), u, om_ref[p, block(r), :])
            put(lam, out, r)
            put_crossing(out_ref, out, p, r, -1)

        loop(body, 2)

    return turn_edge


def relax_edges(ready_f, got_f, state_f, ready_n, got_n, state_n, om_ref, post_f, post_n, out_f, out_n):
    def body(r):
        for p, ready, got, state, post, out_ref in (
            (FAR, ready_f, got_f, state_f, post_f, out_f),
            (NEAR, ready_n, got_n, state_n, post_n, out_n),
        ):
            f = edge_values(ready, got, p, r, 1)
            *u, rho = get(state, r, count=4)
            out = relaxed(f, rho, u, om_ref[p, block(r), :])
            put(post, out, r)
            put_crossing(out_ref, out, p, r, 1)

    loop(body)


def finish(
    far, inner, near, om_ref, u_ref, un_ref, other, post_f, post_i, post_n, other_f, other_n,
    grad, ready_f, final, flat, hold, sem, hold_sem, near_sem, lam, ready_n, got,
):
    parts, posts, m = (far, inner, near), (post_f, post_i, post_n), iotas()

    def run(flip):
        def copy(i, p):
            return pltpu.make_async_copy(
                lam.at[:, i], grad.at[:, :, place(flip, p), :], hold_sem.at[i]
            )

        def stream(r):
            for p in range(PLANES):
                f = pull_local(posts, p, r, 1, m)
                if p not in INNER:
                    pull_remote(other_f if p == FAR else other_n, f, p, r, 1, m)
                put_native(flat, f, flip, p, r)

        def streams(r, carry):
            for j in range(STEP):
                stream(STEP * r + j)
            for j in range(STEP):
                moved(flat, final, sem, STEP * r + j).start()
            return carry

        def body(r):
            for i, p in enumerate(INNER):
                mu = pull_local(parts, p, r, -1, m)
                out = adjoint(mu, get(u_ref, r, (i,), 3), om_ref[p, block(r), :])
                put_mirrored(lam, out, flip, r, (i,))
            for p, ready in ((FAR, ready_f), (NEAR, ready_n)):
                put(ready, pull_local(parts, p, r, -1, m), r)

        lax.fori_loop(0, BLOCKS // STEP, streams, 0)
        loop(body, STEP)
        for i, p in enumerate(INNER):
            copy(i, p).start()
        receive(other, got, NEAR, -1)
        edge_last(ready_n, got, om_ref, un_ref, grad, hold, near_sem, NEAR, flip)
        for i, p in enumerate(INNER):
            copy(i, p).wait()
        loop(lambda r: moved(flat, final, sem, r).wait())

    by_side(run)


def edge_last(ready, got, om_ref, u_ref, grad, hold, sem, p, flip):
    half = ROWS // 2

    def copy(i):
        rows = pl.ds(i * half, half)
        return pltpu.make_async_copy(
            hold.at[:, rows, :], grad.at[:, rows, place(flip, p), :], sem.at[i]
        )

    def body(r):
        mu = edge_values(ready, got, p, r, -1)
        out = adjoint(mu, get(u_ref, r, count=3), om_ref[p, block(r), :])
        put_mirrored(hold, out, flip, r)

    def pairs(first):
        def pair(r, carry):
            body(first + 2 * r)
            body(first + 2 * r + 1)
            return carry

        lax.fori_loop(0, BLOCKS // 4, pair, 0)

    pairs(0)
    copy(0).start()
    pairs(BLOCKS // 2)
    copy(1).start()
    copy(0).wait()
    copy(1).wait()


def far_last(ready, other, om_ref, u_ref, partial, grad, hold, sem, got):
    receive(other, got, FAR, -1)
    by_side(lambda flip: edge_last(ready, got, om_ref, u_ref, grad, hold, sem, FAR, flip))


INSIDE = pl.BlockSpec(memory_space=pltpu.VMEM)
OUTSIDE = pl.BlockSpec(memory_space=pltpu.HBM)
STEP = 2
INNERS = (19, 2, ROWS, LANES)
PLANE = (19, ROWS, LANES)
RELAX = (PLANES, ROWS, LANES)
CROSS = (5, ROWS, LANES)
NATIVE = (19, PLANES * ROWS, LANES)
RESULT = (19, ROWS, PLANES, LANES)
SEMS = pltpu.SemaphoreType.DMA((BLOCKS,))
GOT = [pltpu.VMEM(CROSS, F32)]


def kernel(body, outs, scratch=(), aliases=None):
    def call(*args):
        args = [x if isinstance(x, tuple) else (x, 1) for x in args]
        return pl.pallas_call(
            body,
            in_specs=[INSIDE if inside else OUTSIDE for _, inside in args],
            out_specs=[INSIDE if inside else OUTSIDE for _, inside in outs],
            out_shape=[
                pltpu.VMEM(s, F32) if inside else jax.ShapeDtypeStruct(s, F32) for s, inside in outs
            ],
            scratch_shapes=list(scratch),
            input_output_aliases=aliases or {},
            compiler_params=pltpu.CompilerParams(vmem_limit_bytes=12 * 2**20),
            name=body.__name__,
        )(
            *[
                pltpu.with_memory_space_constraint(x, pltpu.VMEM if inside else pltpu.HBM)
                for x, inside in args
            ]
        )

    return call


def local(populations, relax_class, cotangent):
    count = lax.axis_size("gx")
    near_pairs = [(i, i ^ 1) for i in range(count)]
    far_pairs = [(i, (i + 1 if i % 2 else i - 1) % count) for i in range(count)]

    def exchange(far, near):
        near = lax.ppermute(near, "gx", near_pairs)
        return lax.ppermute(far, "gx", far_pairs), near

    def to_native(x):
        lead = x.shape[:-2]
        x = x.reshape(lead + (PLANES, ROWS, LANES))
        return jnp.swapaxes(x, -3, -2).reshape(lead + (PLANES * ROWS, LANES))

    pops, classes, cot = to_native(populations), to_native(relax_class), to_native(cotangent)
    inners, plane, cross = (INNERS, 1), (PLANE, 1), (CROSS, 1)
    speed, speeds, state = ((3, ROWS, LANES), 1), ((3, 2, ROWS, LANES), 1), ((4, ROWS, LANES), 1)
    held, om, post_f, post_n, u0_f, u0_n, far, near = kernel(
        first_edges,
        [(NATIVE, 1), (RELAX, 1), plane, plane, speed, speed, cross, cross],
        [pltpu.VMEM(classes.shape, jnp.int32), SEMS, pltpu.SemaphoreType.DMA],
    )((pops, 0), (classes, 0))
    cot, far, near = lax.optimization_barrier((cot, far, near))
    far, near = exchange(far, near)
    cot_f, cot_i, cot_n, cfar, cnear = kernel(cotangent_planes, [plane, inners, plane, cross, cross])(
        cot
    )
    cfar, cnear = exchange(cfar, cnear)
    post_i, u0_i = kernel(first_inner, [inners, speeds])(held, om)
    inner = kernel(forward_inner, [inners, speeds, plane, plane])

    post_i, u1_i, ready_f, ready_n = inner(post_f, post_i, post_n, om)
    post_f, post_n, u1_f, u1_n, far, near = kernel(
        forward_edges, [plane, plane, speed, speed, cross, cross], GOT + GOT
    )(ready_f, ready_n, far, near, om)
    far, near = exchange(far, near)
    post_i, u2_i, ready_f, ready_n = inner(post_f, post_i, post_n, om)
    lam_i, mus_f, mus_n = kernel(adjoint_top, [inners, plane, plane])(
        cot_f, cot_i, cot_n, om, u2_i, cfar, cnear
    )
    turn = [kernel(turn_edge(p), [plane, cross, cross, state]) for p in (FAR, NEAR)]
    lam_n, near, got_n, state_n = turn[1](ready_n, near, om, mus_n)
    lam_f, far, got_f, state_f = turn[0](ready_f, far, om, mus_f)
    far, near = exchange(far, near)
    post_f, post_n, pfar, pnear = kernel(relax_edges, [plane, plane, cross, cross])(
        ready_f, got_f, state_f, ready_n, got_n, state_n, om
    )
    lam_i, ready_f, ready_n = kernel(adjoint_inner, [inners, plane, plane])(
        lam_f, lam_i, lam_n, om, u1_i
    )
    pfar, pnear = exchange(pfar, pnear)
    edge = [kernel(adjoint_edge(p), [plane, cross], GOT) for p in (FAR, NEAR)]
    lam_n, near = edge[1](ready_n, near, om, u1_n)
    lam_f, far = edge[0](ready_f, far, om, u1_f)
    far, near = exchange(far, near)
    pair_sem = pltpu.SemaphoreType.DMA((2,))
    grad, ready_f, final = kernel(
        finish,
        [(RESULT, 0), plane, (NATIVE, 0)],
        [pltpu.VMEM(NATIVE, F32), pltpu.VMEM(PLANE, F32), SEMS, pair_sem, pair_sem]
        + [pltpu.VMEM(INNERS, F32), pltpu.VMEM(PLANE, F32)]
        + GOT,
    )(lam_f, lam_i, lam_n, om, u0_i, u0_n, near, post_f, post_i, post_n, pfar, pnear)
    (grad,) = kernel(far_last, [(RESULT, 0)], [pltpu.VMEM(PLANE, F32), pair_sem] + GOT, {4: 0})(
        ready_f, far, om, u0_f, (grad, 0)
    )
    final = jnp.swapaxes(final.reshape(19, ROWS, PLANES, LANES), 1, 2)
    return final.reshape(populations.shape), jnp.swapaxes(grad, 1, 2).reshape(populations.shape)


def solution(mesh):
    return jax.shard_map(
        local,
        mesh=mesh,
        in_specs=(
            P(None, ("groups", "gx"), None),
            P(("groups", "gx"), None),
            P(None, ("groups", "gx"), None),
        ),
        out_specs=(P(None, ("groups", "gx"), None), P(None, ("groups", "gx"), None)),
        check_vma=False,
    )
```

```python
import jax
import jax.numpy as jnp
from jax import lax
from jax.experimental import pallas as pl
from jax.experimental.pallas import tpu as pltpu
from jax.sharding import PartitionSpec as P

PLANES, ROWS, LANES, BLOCKS = 4, 64, 128, 8
SPEEDS = [
    (0, 0, 0), (1, 0, 0), (-1, 0, 0), (0, 1, 0), (0, -1, 0), (0, 0, 1), (0, 0, -1),
    (1, 1, 0), (-1, -1, 0), (1, -1, 0), (-1, 1, 0), (1, 0, 1), (-1, 0, -1),
    (1, 0, -1), (-1, 0, 1), (0, 1, 1), (0, -1, -1), (0, 1, -1), (0, -1, 1),
]
RATES = [1.0 / 1.0, 1.0 / 1.25, 1.0 / 1.6, 1.0 / 2.4]
MIRROR = [SPEEDS.index((-cx, cy, cz)) for cx, cy, cz in SPEEDS]
PLUS = [k for k in range(19) if SPEEDS[k][0] == 1]
MINUS = [MIRROR[k] for k in PLUS]
F32 = jnp.float32


def iotas():
    lane = lax.broadcasted_iota(jnp.int32, (8, LANES), 1)
    row = lax.broadcasted_iota(jnp.int32, (8, LANES), 0)
    turns = {}
    for turn in (0, 64):
        for cz in (1, -1):
            turns[turn, cz] = ((lane & 64) ^ turn) | ((lane - cz) & 63)
    return {"high": lane >= 64, "top": row == 0, "bottom": row == 7, **turns}


def block(r):
    return pl.ds(r * 8 if isinstance(r, int) else pl.multiple_of(r * 8, 8), 8)


def shifted(ref, index, r, cy, cz, m):
    here = ref[index + (block(r), slice(None))]
    turn = 0
    if cy == 1:
        edge = ref[index + (pl.ds(((r + 7) & 7) * 8 + 7, 1), slice(None))]
        other = jnp.where(m["top"], edge, pltpu.roll(here, 1, 0))
        here, turn = jnp.where(m["high"], other, here), 64
    elif cy == -1:
        edge = ref[index + (pl.ds(((r + 1) & 7) * 8, 1), slice(None))]
        other = jnp.where(m["bottom"], edge, pltpu.roll(here, 7, 0))
        here, turn = jnp.where(m["high"], here, other), 64
    if cz == 0:
        return pltpu.roll(here, turn, 1) if turn else here
    return jnp.take_along_axis(here, m[turn, cz], axis=1)


def moments(f):
    s = [f[k] + f[k + 1] for k in range(1, 19, 2)]
    d = [f[k] - f[k + 1] for k in range(1, 19, 2)]
    rho = f[0] + ((s[0] + s[1]) + (s[2] + s[3])) + ((s[4] + s[5]) + (s[6] + s[7])) + s[8]
    jx = d[0] + ((d[3] + d[4]) + (d[5] + d[6]))
    jy = d[1] + ((d[3] - d[4]) + (d[7] + d[8]))
    jz = d[2] + ((d[5] - d[6]) + (d[7] - d[8]))
    return rho, jx, jy, jz


def along_odd(k, v):
    total = None
    for c, x in zip(SPEEDS[k], v):
        if c:
            total = x if total is None else (total + x if c == 1 else total - x)
    return total


def relaxed(f, rho, u, om):
    keep = 1.0 - om
    wr = om * rho
    shape = 1.0 - 1.5 * (u[0] * u[0] + u[1] * u[1] + u[2] * u[2])
    out = [None] * 19
    out[0] = keep * f[0] + (wr * (1.0 / 3.0)) * shape
    for first, last, w in ((1, 7, 1.0 / 18.0), (7, 19, 1.0 / 36.0)):
        part = wr * w
        base, lin, quad = part * shape, part * 3.0, part * 4.5
        for k in range(first, last, 2):
            a = along_odd(k, u)
            even, odd = base + quad * (a * a), lin * a
            out[k] = keep * f[k] + (even + odd)
            out[k + 1] = keep * f[k + 1] + (even - odd)
    return out


def adjoint(mu, u, om):
    s = [None] + [mu[k] + mu[k + 1] for k in range(1, 19, 2)]
    d = [None] + [mu[k] - mu[k + 1] for k in range(1, 19, 2)]
    a, b = 1.0 / 18.0, 1.0 / 36.0
    s45, s67, s89 = s[4] + s[5], s[6] + s[7], s[8] + s[9]
    xx = a * s[1] + b * (s45 + s67)
    yy = a * s[2] + b * (s45 + s89)
    zz = a * s[3] + b * (s67 + s89)
    m0 = (1.0 / 3.0) * mu[0] + a * ((s[1] + s[2]) + s[3]) + b * ((s45 + s67) + s89)
    xy, xz, yz = b * (s[4] - s[5]), b * (s[6] - s[7]), b * (s[8] - s[9])
    mx = a * d[1] + b * ((d[4] + d[5]) + (d[6] + d[7]))
    my = a * d[2] + b * ((d[4] - d[5]) + (d[8] + d[9]))
    mz = a * d[3] + b * ((d[6] - d[7]) + (d[8] - d[9]))
    vx = xx * u[0] + xy * u[1] + xz * u[2]
    vy = xy * u[0] + yy * u[1] + yz * u[2]
    vz = xz * u[0] + yz * u[1] + zz * u[2]
    uu = u[0] * u[0] + u[1] * u[1] + u[2] * u[2]
    rho_part = om * (m0 + 1.5 * (m0 * uu) - 4.5 * (u[0] * vx + u[1] * vy + u[2] * vz))
    om3 = 3.0 * om
    flow = [
        om3 * (mx + 3.0 * vx - u[0] * m0),
        om3 * (my + 3.0 * vy - u[1] * m0),
        om3 * (mz + 3.0 * vz - u[2] * m0),
    ]
    keep = 1.0 - om
    out = [None] * 19
    out[0] = keep * mu[0] + rho_part
    for k in range(1, 19, 2):
        g = along_odd(k, flow)
        out[k] = keep * mu[k] + (rho_part + g)
        out[k + 1] = keep * mu[k + 1] + (rho_part - g)
    return out


FAR, NEAR, INNER = 0, PLANES - 1, (1, 2)


def plane_of(parts, p):
    far, inner, near = parts
    return (far, ()) if p == FAR else (near, ()) if p == NEAR else (inner, (INNER.index(p),))


def pull_local(parts, p, r, sign, m):
    out = [None] * 19
    for k in range(19):
        cx, cy, cz = (sign * c for c in SPEEDS[k])
        if 0 <= p - cx < PLANES:
            ref, i = plane_of(parts, p - cx)
            out[k] = shifted(ref, (k,) + i, r, cy, cz, m)
    return out


def crossing(p, sign):
    return (PLUS, MINUS)[(sign == 1) != (p == FAR)]


def pull_remote(other, out, p, r, sign, m):
    for i, k in enumerate(crossing(p, sign)):
        out[k] = shifted(other, (i,), r, sign * SPEEDS[k][1], sign * SPEEDS[k][2], m)
    return out


def put(ref, values, r, i=()):
    for k, value in enumerate(values):
        if value is not None:
            ref[(k,) + i + (block(r), slice(None))] = value


def get(ref, r, i=(), count=19, missing=()):
    return [
        None if k in missing else ref[(k,) + i + (block(r), slice(None))] for k in range(count)
    ]


def put_crossing(ref, values, p, r, sign):
    put(ref, [values[k] for k in crossing(p, -sign)], r)


def state_of(f):
    rho, jx, jy, jz = moments(f)
    inv = 1.0 / rho
    return rho, [jx * inv, jy * inv, jz * inv]


def by_side(run):
    side = lax.rem(lax.axis_index("gx"), 2)
    for flip in (0, 1):
        pl.when(side == flip)(lambda flip=flip: run(flip))


def native(flip, k, p, r):
    return mirrored(flip, k), pl.ds(r * (8 * PLANES) + place(flip, p), 8, stride=PLANES)


def mirrored(flip, k):
    return MIRROR[k] if flip else k


def place(flip, p):
    return PLANES - 1 - p if flip else p


def get_native(ref, flip, p, r):
    out = []
    for k in range(19):
        kk, rows = native(flip, k, p, r)
        out.append(ref[kk, rows, :])
    return out


def put_native(ref, values, flip, p, r):
    for k in range(19):
        kk, rows = native(flip, k, p, r)
        ref[kk, rows, :] = values[k]


def put_mirrored(hold, values, flip, r, i=()):
    for k in range(19):
        hold[(mirrored(flip, k),) + i + (block(r), slice(None))] = values[k]


def loop(body, step=1):
    def steps(r, carry):
        for j in range(step):
            body(r * step + j)
        return carry

    lax.fori_loop(0, BLOCKS // step, steps, 0)


def chunk(ref, r):
    rows = 8 * PLANES
    return ref.at[:, pl.ds(pl.multiple_of(r * rows, rows), rows), :]


def moved(source, target, sem, r):
    return pltpu.make_async_copy(chunk(source, r), chunk(target, r), sem.at[r])


def first_edges(
    pops, classes, held, om_ref, post_f, post_n, u_f, u_n, far_out, near_out, cls_ref, sem, cls_sem
):
    fetch = pltpu.make_async_copy(classes, cls_ref, cls_sem)
    fetch.start()
    loop(lambda r: moved(pops, held, sem, r).start())
    fetch.wait()

    def run(flip):
        def body(r):
            moved(pops, held, sem, r).wait()
            for p in range(PLANES):
                cls = cls_ref[native(flip, 0, p, r)[1], :]
                om = jnp.full((8, LANES), RATES[0], F32)
                for entry in range(1, 4):
                    om = jnp.where(cls == entry, RATES[entry], om)
                om_ref[p, block(r), :] = om
                if p in INNER:
                    continue
                f = get_native(held, flip, p, r)
                rho, u = state_of(f)
                put(u_f if p == FAR else u_n, u, r)
                out = relaxed(f, rho, u, om)
                put(post_f if p == FAR else post_n, out, r)
                put_crossing(far_out if p == FAR else near_out, out, p, r, 1)

        loop(body)

    by_side(run)


def first_inner(held, om_ref, post, u_ref):
    def run(flip):
        def body(r):
            for i, p in enumerate(INNER):
                f = get_native(held, flip, p, r)
                rho, u = state_of(f)
                put(u_ref, u, r, (i,))
                put(post, relaxed(f, rho, u, om_ref[p, block(r), :]), r, (i,))

        loop(body)

    by_side(run)


def cotangent_planes(cot, far, inner, near, far_out, near_out):
    def run(flip):
        def body(r):
            for p in range(PLANES):
                values = get_native(cot, flip, p, r)
                ref, i = plane_of((far, inner, near), p)
                put(ref, values, r, i)
                if p not in INNER:
                    put_crossing(far_out if p == FAR else near_out, values, p, r, -1)

        loop(body)

    by_side(run)


def forward_inner(far, inner, near, om_ref, post, u_ref, ready_f, ready_n):
    parts, m = (far, inner, near), iotas()

    def body(r):
        for i, p in enumerate(INNER):
            f = pull_local(parts, p, r, 1, m)
            rho, u = state_of(f)
            put(u_ref, u, r, (i,))
            put(post, relaxed(f, rho, u, om_ref[p, block(r), :]), r, (i,))
        for p, ready in ((FAR, ready_f), (NEAR, ready_n)):
            put(ready, pull_local(parts, p, r, 1, m), r)

    loop(body, STEP)


def receive(other, got, p, sign):
    m = iotas()
    for r in range(BLOCKS):
        for j, k in enumerate(crossing(p, sign)):
            cy, cz = sign * SPEEDS[k][1], sign * SPEEDS[k][2]
            got[j, block(r), :] = shifted(other, (j,), r, cy, cz, m)


def edge_values(ready, got, p, r, sign):
    values = get(ready, r, missing=crossing(p, sign))
    for j, k in enumerate(crossing(p, sign)):
        values[k] = got[j, block(r), :]
    return values


def forward_edges(
    ready_f, ready_n, far, near, om_ref,
    post_f, post_n, u_f, u_n, out_f, out_n, got_f, got_n,
):
    sides = (
        (FAR, ready_f, far, post_f, u_f, out_f, got_f),
        (NEAR, ready_n, near, post_n, u_n, out_n, got_n),
    )
    for p, _, other, _, _, _, got in sides:
        receive(other, got, p, 1)

    def body(r):
        for p, ready, _, post, u_ref, out_ref, got in sides:
            f = edge_values(ready, got, p, r, 1)
            rho, u = state_of(f)
            put(u_ref, u, r)
            out = relaxed(f, rho, u, om_ref[p, block(r), :])
            put(post, out, r)
            put_crossing(out_ref, out, p, r, 1)

    loop(body)


def adjoint_planes(parts, om_ref, u_ref, lam, r, m):
    for i, p in enumerate(INNER):
        mu = pull_local(parts, p, r, -1, m)
        out = adjoint(mu, get(u_ref, r, (i,), 3), om_ref[p, block(r), :])
        put(lam, out, r, (i,))


def write_half(hold, result, sem, flip, p, i):
    rows = pl.ds(i * (ROWS // 2), ROWS // 2)
    return pltpu.make_async_copy(
        hold.at[:, rows, :], result.at[:, rows, place(flip, p), :], sem.at[i]
    )


def by_halves(body, after):
    for i in range(2):
        first = i * (BLOCKS // 2)

        def pair(r, carry, first=first):
            body(first + 2 * r)
            body(first + 2 * r + 1)
            return carry

        lax.fori_loop(0, BLOCKS // 4, pair, 0)
        after(i)


def stream_planes(places, posts, others, result, flip, m):
    def body(r):
        for p, hold, _ in places:
            f = pull_local(posts, p, r, 1, m)
            if p not in INNER:
                pull_remote(others[p == NEAR], f, p, r, 1, m)
            put_mirrored(hold, f, flip, r)

    def after(i):
        for p, hold, sem in places:
            write_half(hold, result, sem, flip, p, i).start()

    by_halves(body, after)


def wait_planes(places, result, flip):
    for p, hold, sem in places:
        for i in range(2):
            write_half(hold, result, sem, flip, p, i).wait()


def adjoint_inner(
    far, inner, near, om_ref, u_ref, post_f, post_i, post_n,
    lam, ready_f, ready_n, final, hold_1, hold_2, sem_1, sem_2,
):
    parts, m = (far, inner, near), iotas()
    places = ((1, hold_1, sem_1), (2, hold_2, sem_2))
    by_side(lambda flip: stream_planes(places, (post_f, post_i, post_n), None, final, flip, m))

    def body(r):
        adjoint_planes(parts, om_ref, u_ref, lam, r, m)
        for p, ready in ((FAR, ready_f), (NEAR, ready_n)):
            put(ready, pull_local(parts, p, r, -1, m), r)

    loop(body, STEP)
    by_side(lambda flip: wait_planes(places, final, flip))


def adjoint_top(far, inner, near, om_ref, u_ref, other_f, other_n, lam, mus_f, mus_n):
    parts, m = (far, inner, near), iotas()

    def body(r):
        adjoint_planes(parts, om_ref, u_ref, lam, r, m)
        for p, mus, other in ((FAR, mus_f, other_f), (NEAR, mus_n, other_n)):
            put(mus, pull_remote(other, pull_local(parts, p, r, -1, m), p, r, -1, m), r)

    loop(body, STEP)


def adjoint_edge(p):
    def adjoint_edge(ready, other, om_ref, u_ref, lam, out_ref, got):
        receive(other, got, p, -1)

        def body(r):
            mu = edge_values(ready, got, p, r, -1)
            out = adjoint(mu, get(u_ref, r, count=3), om_ref[p, block(r), :])
            put(lam, out, r)
            put_crossing(out_ref, out, p, r, -1)

        loop(body, 2)

    return adjoint_edge


def turn_edge(p):
    def turn_edge(ready, other, om_ref, mus, lam, out_ref, got, state):
        receive(other, got, p, 1)

        def body(r):
            rho, u = state_of(edge_values(ready, got, p, r, 1))
            put(state, u + [rho], r)
            out = adjoint(get(mus, r), u, om_ref[p, block(r), :])
            put(lam, out, r)
            put_crossing(out_ref, out, p, r, -1)

        loop(body, 2)

    return turn_edge


def relax_edges(ready_f, got_f, state_f, ready_n, got_n, state_n, om_ref, post_f, post_n, out_f, out_n):
    def body(r):
        for p, ready, got, state, post, out_ref in (
            (FAR, ready_f, got_f, state_f, post_f, out_f),
            (NEAR, ready_n, got_n, state_n, post_n, out_n),
        ):
            f = edge_values(ready, got, p, r, 1)
            *u, rho = get(state, r, count=4)
            out = relaxed(f, rho, u, om_ref[p, block(r), :])
            put(post, out, r)
            put_crossing(out_ref, out, p, r, 1)

    loop(body)


def finish(
    far, inner, near, om_ref, u_ref, un_ref, other, post_f, post_i, post_n, other_f, other_n, partial,
    grad, ready_f, final, hold_1, hold_2, sem_1, sem_2, hold, hold_sem, near_sem, lam, ready_n, got,
):
    parts, posts, m = (far, inner, near), (post_f, post_i, post_n), iotas()
    places = ((FAR, hold_1, sem_1), (NEAR, hold_2, sem_2))

    def run(flip):
        def copy(i, p):
            return pltpu.make_async_copy(
                lam.at[:, i], grad.at[:, :, place(flip, p), :], hold_sem.at[i]
            )

        def body(r):
            for i, p in enumerate(INNER):
                mu = pull_local(parts, p, r, -1, m)
                out = adjoint(mu, get(u_ref, r, (i,), 3), om_ref[p, block(r), :])
                put_mirrored(lam, out, flip, r, (i,))
            for p, ready in ((FAR, ready_f), (NEAR, ready_n)):
                put(ready, pull_local(parts, p, r, -1, m), r)

        stream_planes(places, posts, (other_f, other_n), final, flip, m)
        loop(body, STEP)
        for i, p in enumerate(INNER):
            copy(i, p).start()
        edge_last(ready_n, other, got, om_ref, un_ref, grad, hold, near_sem, NEAR, flip)
        for i, p in enumerate(INNER):
            copy(i, p).wait()
        wait_planes(places, final, flip)

    by_side(run)


def edge_last(ready, other, got, om_ref, u_ref, grad, hold, sem, p, flip):
    receive(other, got, p, -1)

    def body(r):
        mu = edge_values(ready, got, p, r, -1)
        out = adjoint(mu, get(u_ref, r, count=3), om_ref[p, block(r), :])
        put_mirrored(hold, out, flip, r)

    by_halves(body, lambda i: write_half(hold, grad, sem, flip, p, i).start())
    for i in range(2):
        write_half(hold, grad, sem, flip, p, i).wait()


def far_last(ready, other, om_ref, u_ref, partial, grad, hold, sem, got):
    by_side(
        lambda flip: edge_last(ready, other, got, om_ref, u_ref, grad, hold, sem, FAR, flip)
    )


INSIDE = pl.BlockSpec(memory_space=pltpu.VMEM)
OUTSIDE = pl.BlockSpec(memory_space=pltpu.HBM)
STEP = 2
INNERS = (19, 2, ROWS, LANES)
PLANE = (19, ROWS, LANES)
RELAX = (PLANES, ROWS, LANES)
CROSS = (5, ROWS, LANES)
NATIVE = (19, PLANES * ROWS, LANES)
RESULT = (19, ROWS, PLANES, LANES)
SEMS = pltpu.SemaphoreType.DMA((BLOCKS,))
GOT = [pltpu.VMEM(CROSS, F32)]


def kernel(body, outs, scratch=(), aliases=None):
    def call(*args):
        args = [x if isinstance(x, tuple) else (x, 1) for x in args]
        return pl.pallas_call(
            body,
            in_specs=[INSIDE if inside else OUTSIDE for _, inside in args],
            out_specs=[INSIDE if inside else OUTSIDE for _, inside in outs],
            out_shape=[
                pltpu.VMEM(s, F32) if inside else jax.ShapeDtypeStruct(s, F32) for s, inside in outs
            ],
            scratch_shapes=list(scratch),
            input_output_aliases=aliases or {},
            compiler_params=pltpu.CompilerParams(vmem_limit_bytes=12 * 2**20),
            name=body.__name__,
        )(
            *[
                pltpu.with_memory_space_constraint(x, pltpu.VMEM if inside else pltpu.HBM)
                for x, inside in args
            ]
        )

    return call


def local(populations, relax_class, cotangent):
    count = lax.axis_size("gx")
    near_pairs = [(i, i ^ 1) for i in range(count)]
    far_pairs = [(i, (i + 1 if i % 2 else i - 1) % count) for i in range(count)]

    def exchange(far, near):
        near = lax.ppermute(near, "gx", near_pairs)
        return lax.ppermute(far, "gx", far_pairs), near

    def to_native(x):
        lead = x.shape[:-2]
        x = x.reshape(lead + (PLANES, ROWS, LANES))
        return jnp.swapaxes(x, -3, -2).reshape(lead + (PLANES * ROWS, LANES))

    pops, classes, cot = to_native(populations), to_native(relax_class), to_native(cotangent)
    inners, plane, cross = (INNERS, 1), (PLANE, 1), (CROSS, 1)
    speed, speeds, state = ((3, ROWS, LANES), 1), ((3, 2, ROWS, LANES), 1), ((4, ROWS, LANES), 1)
    held, om, post_f, post_n, u0_f, u0_n, far, near = kernel(
        first_edges,
        [(NATIVE, 1), (RELAX, 1), plane, plane, speed, speed, cross, cross],
        [pltpu.VMEM(classes.shape, jnp.int32), SEMS, pltpu.SemaphoreType.DMA],
    )((pops, 0), (classes, 0))
    cot, far, near = lax.optimization_barrier((cot, far, near))
    far, near = exchange(far, near)
    cot_f, cot_i, cot_n, cfar, cnear = kernel(cotangent_planes, [plane, inners, plane, cross, cross])(
        cot
    )
    cfar, cnear = exchange(cfar, cnear)
    post_i, u0_i = kernel(first_inner, [inners, speeds])(held, om)
    inner = kernel(forward_inner, [inners, speeds, plane, plane])

    post_i, u1_i, ready_f, ready_n = inner(post_f, post_i, post_n, om)
    post_f, post_n, u1_f, u1_n, far, near = kernel(
        forward_edges, [plane, plane, speed, speed, cross, cross], GOT + GOT
    )(ready_f, ready_n, far, near, om)
    far, near = exchange(far, near)
    post_i, u2_i, ready_f, ready_n = inner(post_f, post_i, post_n, om)
    lam_i, mus_f, mus_n = kernel(adjoint_top, [inners, plane, plane])(
        cot_f, cot_i, cot_n, om, u2_i, cfar, cnear
    )
    turn = [kernel(turn_edge(p), [plane, cross, cross, state]) for p in (FAR, NEAR)]
    lam_n, near, got_n, state_n = turn[1](ready_n, near, om, mus_n)
    lam_f, far, got_f, state_f = turn[0](ready_f, far, om, mus_f)
    far, near = exchange(far, near)
    post_f, post_n, pfar, pnear = kernel(relax_edges, [plane, plane, cross, cross])(
        ready_f, got_f, state_f, ready_n, got_n, state_n, om
    )
    pair_sem = pltpu.SemaphoreType.DMA((2,))
    halves = [pltpu.VMEM(PLANE, F32), pltpu.VMEM(PLANE, F32), pair_sem, pair_sem]
    lam_i, ready_f, ready_n, final = kernel(
        adjoint_inner, [inners, plane, plane, (RESULT, 0)], halves
    )(lam_f, lam_i, lam_n, om, u1_i, post_f, post_i, post_n)
    pfar, pnear, ready_f = lax.optimization_barrier((pfar, pnear, ready_f))
    pfar, pnear = exchange(pfar, pnear)
    edge = [kernel(adjoint_edge(p), [plane, cross], GOT) for p in (FAR, NEAR)]
    lam_n, near = edge[1](ready_n, near, om, u1_n)
    lam_f, far = edge[0](ready_f, far, om, u1_f)
    far, near = exchange(far, near)
    grad, ready_f, final = kernel(
        finish,
        [(RESULT, 0), plane, (RESULT, 0)],
        halves
        + [pltpu.VMEM(PLANE, F32), pair_sem, pair_sem, pltpu.VMEM(INNERS, F32), pltpu.VMEM(PLANE, F32)]
        + GOT,
        {12: 2},
    )(lam_f, lam_i, lam_n, om, u0_i, u0_n, near, post_f, post_i, post_n, pfar, pnear, (final, 0))
    (grad,) = kernel(far_last, [(RESULT, 0)], [pltpu.VMEM(PLANE, F32), pair_sem] + GOT, {4: 0})(
        ready_f, far, om, u0_f, (grad, 0)
    )
    return tuple(jnp.swapaxes(x, 1, 2).reshape(populations.shape) for x in (final, grad))


def solution(mesh):
    return jax.shard_map(
        local,
        mesh=mesh,
        in_specs=(
            P(None, ("groups", "gx"), None),
            P(("groups", "gx"), None),
            P(None, ("groups", "gx"), None),
        ),
        out_specs=(P(None, ("groups", "gx"), None), P(None, ("groups", "gx"), None)),
        check_vma=False,
    )
```

```python
import jax
import jax.numpy as jnp
from jax import lax
from jax.experimental import pallas as pl
from jax.experimental.pallas import tpu as pltpu
from jax.sharding import PartitionSpec as P

PLANES, ROWS, LANES, BLOCKS = 4, 64, 128, 8
SPEEDS = [
    (0, 0, 0), (1, 0, 0), (-1, 0, 0), (0, 1, 0), (0, -1, 0), (0, 0, 1), (0, 0, -1),
    (1, 1, 0), (-1, -1, 0), (1, -1, 0), (-1, 1, 0), (1, 0, 1), (-1, 0, -1),
    (1, 0, -1), (-1, 0, 1), (0, 1, 1), (0, -1, -1), (0, 1, -1), (0, -1, 1),
]
RATES = [1.0 / 1.0, 1.0 / 1.25, 1.0 / 1.6, 1.0 / 2.4]
MIRROR = [SPEEDS.index((-cx, cy, cz)) for cx, cy, cz in SPEEDS]
PLUS = [k for k in range(19) if SPEEDS[k][0] == 1]
MINUS = [MIRROR[k] for k in PLUS]
F32 = jnp.float32


def iotas():
    lane = lax.broadcasted_iota(jnp.int32, (8, LANES), 1)
    row = lax.broadcasted_iota(jnp.int32, (8, LANES), 0)
    turns = {}
    for turn in (0, 64):
        for cz in (1, -1):
            turns[turn, cz] = ((lane & 64) ^ turn) | ((lane - cz) & 63)
    return {"high": lane >= 64, "top": row == 0, "bottom": row == 7, **turns}


def block(r):
    return pl.ds(r * 8 if isinstance(r, int) else pl.multiple_of(r * 8, 8), 8)


def shifted(ref, index, r, cy, cz, m):
    here = ref[index + (block(r), slice(None))]
    turn = 0
    if cy == 1:
        edge = ref[index + (pl.ds(((r + 7) & 7) * 8 + 7, 1), slice(None))]
        other = jnp.where(m["top"], edge, pltpu.roll(here, 1, 0))
        here, turn = jnp.where(m["high"], other, here), 64
    elif cy == -1:
        edge = ref[index + (pl.ds(((r + 1) & 7) * 8, 1), slice(None))]
        other = jnp.where(m["bottom"], edge, pltpu.roll(here, 7, 0))
        here, turn = jnp.where(m["high"], here, other), 64
    if cz == 0:
        return pltpu.roll(here, turn, 1) if turn else here
    return jnp.take_along_axis(here, m[turn, cz], axis=1)


def moments(f):
    s = [f[k] + f[k + 1] for k in range(1, 19, 2)]
    d = [f[k] - f[k + 1] for k in range(1, 19, 2)]
    rho = f[0] + ((s[0] + s[1]) + (s[2] + s[3])) + ((s[4] + s[5]) + (s[6] + s[7])) + s[8]
    jx = d[0] + ((d[3] + d[4]) + (d[5] + d[6]))
    jy = d[1] + ((d[3] - d[4]) + (d[7] + d[8]))
    jz = d[2] + ((d[5] - d[6]) + (d[7] - d[8]))
    return rho, jx, jy, jz


def along_odd(k, v):
    total = None
    for c, x in zip(SPEEDS[k], v):
        if c:
            total = x if total is None else (total + x if c == 1 else total - x)
    return total


def relaxed(f, rho, u, om):
    keep = 1.0 - om
    wr = om * rho
    shape = 1.0 - 1.5 * (u[0] * u[0] + u[1] * u[1] + u[2] * u[2])
    out = [None] * 19
    out[0] = keep * f[0] + (wr * (1.0 / 3.0)) * shape
    for first, last, w in ((1, 7, 1.0 / 18.0), (7, 19, 1.0 / 36.0)):
        part = wr * w
        base, lin, quad = part * shape, part * 3.0, part * 4.5
        for k in range(first, last, 2):
            a = along_odd(k, u)
            even, odd = base + quad * (a * a), lin * a
            out[k] = keep * f[k] + (even + odd)
            out[k + 1] = keep * f[k + 1] + (even - odd)
    return out


def adjoint(mu, u, om):
    s = [None] + [mu[k] + mu[k + 1] for k in range(1, 19, 2)]
    d = [None] + [mu[k] - mu[k + 1] for k in range(1, 19, 2)]
    a, b = 1.0 / 18.0, 1.0 / 36.0
    s45, s67, s89 = s[4] + s[5], s[6] + s[7], s[8] + s[9]
    xx = a * s[1] + b * (s45 + s67)
    yy = a * s[2] + b * (s45 + s89)
    zz = a * s[3] + b * (s67 + s89)
    m0 = (1.0 / 3.0) * mu[0] + a * ((s[1] + s[2]) + s[3]) + b * ((s45 + s67) + s89)
    xy, xz, yz = b * (s[4] - s[5]), b * (s[6] - s[7]), b * (s[8] - s[9])
    mx = a * d[1] + b * ((d[4] + d[5]) + (d[6] + d[7]))
    my = a * d[2] + b * ((d[4] - d[5]) + (d[8] + d[9]))
    mz = a * d[3] + b * ((d[6] - d[7]) + (d[8] - d[9]))
    vx = xx * u[0] + xy * u[1] + xz * u[2]
    vy = xy * u[0] + yy * u[1] + yz * u[2]
    vz = xz * u[0] + yz * u[1] + zz * u[2]
    uu = u[0] * u[0] + u[1] * u[1] + u[2] * u[2]
    rho_part = om * (m0 + 1.5 * (m0 * uu) - 4.5 * (u[0] * vx + u[1] * vy + u[2] * vz))
    om3 = 3.0 * om
    flow = [
        om3 * (mx + 3.0 * vx - u[0] * m0),
        om3 * (my + 3.0 * vy - u[1] * m0),
        om3 * (mz + 3.0 * vz - u[2] * m0),
    ]
    keep = 1.0 - om
    out = [None] * 19
    out[0] = keep * mu[0] + rho_part
    for k in range(1, 19, 2):
        g = along_odd(k, flow)
        out[k] = keep * mu[k] + (rho_part + g)
        out[k + 1] = keep * mu[k + 1] + (rho_part - g)
    return out


FAR, NEAR, INNER = 0, PLANES - 1, (1, 2)


def plane_of(parts, p):
    far, inner, near = parts
    return (far, ()) if p == FAR else (near, ()) if p == NEAR else (inner, (INNER.index(p),))


def pull_local(parts, p, r, sign, m):
    out = [None] * 19
    for k in range(19):
        cx, cy, cz = (sign * c for c in SPEEDS[k])
        if 0 <= p - cx < PLANES:
            ref, i = plane_of(parts, p - cx)
            out[k] = shifted(ref, (k,) + i, r, cy, cz, m)
    return out


def crossing(p, sign):
    return (PLUS, MINUS)[(sign == 1) != (p == FAR)]


def pull_remote(other, out, p, r, sign, m):
    for i, k in enumerate(crossing(p, sign)):
        out[k] = shifted(other, (i,), r, sign * SPEEDS[k][1], sign * SPEEDS[k][2], m)
    return out


def put(ref, values, r, i=()):
    for k, value in enumerate(values):
        if value is not None:
            ref[(k,) + i + (block(r), slice(None))] = value


def get(ref, r, i=(), count=19, missing=()):
    return [
        None if k in missing else ref[(k,) + i + (block(r), slice(None))] for k in range(count)
    ]


def put_crossing(ref, values, p, r, sign):
    put(ref, [values[k] for k in crossing(p, -sign)], r)


def state_of(f):
    rho, jx, jy, jz = moments(f)
    inv = 1.0 / rho
    return rho, [jx * inv, jy * inv, jz * inv]


def by_side(run):
    side = lax.rem(lax.axis_index("gx"), 2)
    for flip in (0, 1):
        pl.when(side == flip)(lambda flip=flip: run(flip))


def native(flip, k, p, r):
    return mirrored(flip, k), pl.ds(r * (8 * PLANES) + place(flip, p), 8, stride=PLANES)


def mirrored(flip, k):
    return MIRROR[k] if flip else k


def place(flip, p):
    return PLANES - 1 - p if flip else p


def get_native(ref, flip, p, r):
    out = []
    for k in range(19):
        kk, rows = native(flip, k, p, r)
        out.append(ref[kk, rows, :])
    return out


def put_native(ref, values, flip, p, r):
    for k in range(19):
        kk, rows = native(flip, k, p, r)
        ref[kk, rows, :] = values[k]


def put_mirrored(hold, values, flip, r, i=()):
    for k in range(19):
        hold[(mirrored(flip, k),) + i + (block(r), slice(None))] = values[k]


def loop(body, step=1):
    def steps(r, carry):
        for j in range(step):
            body(r * step + j)
        return carry

    lax.fori_loop(0, BLOCKS // step, steps, 0)


def chunk(ref, r):
    rows = 8 * PLANES
    return ref.at[:, pl.ds(pl.multiple_of(r * rows, rows), rows), :]


def moved(source, target, sem, r):
    return pltpu.make_async_copy(chunk(source, r), chunk(target, r), sem.at[r])


def first_edges(
    pops, classes, om_ref, post_f, post_n, u_f, u_n, far_out, near_out, held_f, held_n, cls_ref, sem_f, sem_n, cls_sem
):
    fetch = pltpu.make_async_copy(classes, cls_ref, cls_sem)
    sides = (
        (FAR, held_f, sem_f, post_f, u_f, far_out),
        (NEAR, held_n, sem_n, post_n, u_n, near_out),
    )

    def run(flip):
        def copy(p, held, sem, r):
            return pltpu.make_async_copy(
                pops.at[:, block(r), place(flip, p), :], held.at[:, block(r), :], sem.at[r]
            )

        def start(r):
            for p, held, sem, *_ in sides:
                copy(p, held, sem, r).start()

        def body(r):
            for p in range(PLANES):
                cls = cls_ref[native(flip, 0, p, r)[1], :]
                om = jnp.full((8, LANES), RATES[0], F32)
                for entry in range(1, 4):
                    om = jnp.where(cls == entry, RATES[entry], om)
                om_ref[p, block(r), :] = om
            for p, held, sem, *_ in sides:
                copy(p, held, sem, r).wait()
            for p, held, sem, post, u_ref, out_ref in sides:
                f = [held[mirrored(flip, k), block(r), :] for k in range(19)]
                rho, u = state_of(f)
                put(u_ref, u, r)
                out = relaxed(f, rho, u, om_ref[p, block(r), :])
                put(post, out, r)
                put_crossing(out_ref, out, p, r, 1)

        loop(start)
        fetch.wait()
        loop(body)

    fetch.start()
    by_side(run)


def first_inner(held, om_ref, post, u_ref):
    def run(flip):
        def body(r):
            for i, p in enumerate(INNER):
                f = get_native(held, flip, p, r)
                rho, u = state_of(f)
                put(u_ref, u, r, (i,))
                put(post, relaxed(f, rho, u, om_ref[p, block(r), :]), r, (i,))

        loop(body)

    by_side(run)


def cotangent_planes(cot, far, inner, near, far_out, near_out):
    def run(flip):
        def body(r):
            for p in range(PLANES):
                values = get_native(cot, flip, p, r)
                ref, i = plane_of((far, inner, near), p)
                put(ref, values, r, i)
                if p not in INNER:
                    put_crossing(far_out if p == FAR else near_out, values, p, r, -1)

        loop(body)

    by_side(run)


def forward_inner(far, inner, near, om_ref, post, u_ref, ready_f, ready_n):
    parts, m = (far, inner, near), iotas()

    def body(r):
        for i, p in enumerate(INNER):
            f = pull_local(parts, p, r, 1, m)
            rho, u = state_of(f)
            put(u_ref, u, r, (i,))
            put(post, relaxed(f, rho, u, om_ref[p, block(r), :]), r, (i,))
        for p, ready in ((FAR, ready_f), (NEAR, ready_n)):
            put(ready, pull_local(parts, p, r, 1, m), r)

    loop(body, STEP)


def receive(other, got, p, sign):
    m = iotas()
    for r in range(BLOCKS):
        for j, k in enumerate(crossing(p, sign)):
            cy, cz = sign * SPEEDS[k][1], sign * SPEEDS[k][2]
            got[j, block(r), :] = shifted(other, (j,), r, cy, cz, m)


def edge_values(ready, got, p, r, sign):
    values = get(ready, r, missing=crossing(p, sign))
    for j, k in enumerate(crossing(p, sign)):
        values[k] = got[j, block(r), :]
    return values


def forward_edges(
    ready_f, ready_n, far, near, om_ref,
    post_f, post_n, u_f, u_n, out_f, out_n, got_f, got_n,
):
    sides = (
        (FAR, ready_f, far, post_f, u_f, out_f, got_f),
        (NEAR, ready_n, near, post_n, u_n, out_n, got_n),
    )
    for p, _, other, _, _, _, got in sides:
        receive(other, got, p, 1)

    def body(r):
        for p, ready, _, post, u_ref, out_ref, got in sides:
            f = edge_values(ready, got, p, r, 1)
            rho, u = state_of(f)
            put(u_ref, u, r)
            out = relaxed(f, rho, u, om_ref[p, block(r), :])
            put(post, out, r)
            put_crossing(out_ref, out, p, r, 1)

    loop(body)


def adjoint_planes(parts, om_ref, u_ref, lam, r, m):
    for i, p in enumerate(INNER):
        mu = pull_local(parts, p, r, -1, m)
        out = adjoint(mu, get(u_ref, r, (i,), 3), om_ref[p, block(r), :])
        put(lam, out, r, (i,))


def adjoint_inner(far, inner, near, om_ref, u_ref, lam, ready_f, ready_n):
    parts, m = (far, inner, near), iotas()

    def body(r):
        adjoint_planes(parts, om_ref, u_ref, lam, r, m)
        for p, ready in ((FAR, ready_f), (NEAR, ready_n)):
            put(ready, pull_local(parts, p, r, -1, m), r)

    loop(body, STEP)


def adjoint_top(far, inner, near, om_ref, u_ref, other_f, other_n, lam, mus_f, mus_n):
    parts, m = (far, inner, near), iotas()

    def body(r):
        adjoint_planes(parts, om_ref, u_ref, lam, r, m)
        for p, mus, other in ((FAR, mus_f, other_f), (NEAR, mus_n, other_n)):
            put(mus, pull_remote(other, pull_local(parts, p, r, -1, m), p, r, -1, m), r)

    loop(body, STEP)


def adjoint_edge(p):
    def adjoint_edge(ready, other, om_ref, u_ref, lam, out_ref, got):
        receive(other, got, p, -1)

        def body(r):
            mu = edge_values(ready, got, p, r, -1)
            out = adjoint(mu, get(u_ref, r, count=3), om_ref[p, block(r), :])
            put(lam, out, r)
            put_crossing(out_ref, out, p, r, -1)

        loop(body, 2)

    return adjoint_edge


def turn_edge(p):
    def turn_edge(ready, other, om_ref, mus, lam, out_ref, got, state):
        receive(other, got, p, 1)

        def body(r):
            rho, u = state_of(edge_values(ready, got, p, r, 1))
            put(state, u + [rho], r)
            out = adjoint(get(mus, r), u, om_ref[p, block(r), :])
            put(lam, out, r)
            put_crossing(out_ref, out, p, r, -1)

        loop(body, 2)

    return turn_edge


def relax_edges(ready_f, got_f, state_f, ready_n, got_n, state_n, om_ref, post_f, post_n, out_f, out_n):
    def body(r):
        for p, ready, got, state, post, out_ref in (
            (FAR, ready_f, got_f, state_f, post_f, out_f),
            (NEAR, ready_n, got_n, state_n, post_n, out_n),
        ):
            f = edge_values(ready, got, p, r, 1)
            *u, rho = get(state, r, count=4)
            out = relaxed(f, rho, u, om_ref[p, block(r), :])
            put(post, out, r)
            put_crossing(out_ref, out, p, r, 1)

    loop(body)


def finish(
    far, inner, near, om_ref, u_ref, un_ref, other, post_f, post_i, post_n, other_f, other_n,
    grad, ready_f, final, flat, hold, sem, hold_sem, near_sem, lam, ready_n, even, odd, got,
):
    parts, posts, m = (far, inner, near), (post_f, post_i, post_n), iotas()

    def run(flip):
        def copy(i, p, h):
            rows = pl.ds(h * (ROWS // 2), ROWS // 2)
            return pltpu.make_async_copy(
                lam.at[:, i, rows, :], grad.at[:, rows, place(flip, p), :], hold_sem.at[2 * i + h]
            )

        def stream(r):
            for p in range(PLANES):
                f = pull_local(posts, p, r, 1, m)
                if p not in INNER:
                    pull_remote(other_f if p == FAR else other_n, f, p, r, 1, m)
                put_native(flat, f, flip, p, r)

        def pull(r, keep):
            for i, p in enumerate(INNER):
                for k, value in enumerate(pull_local(parts, p, r, -1, m)):
                    keep[19 * i + k] = value
            for p, ready in ((FAR, ready_f), (NEAR, ready_n)):
                put(ready, pull_local(parts, p, r, -1, m), r)

        def turn(r, keep):
            for i, p in enumerate(INNER):
                mu = [keep[19 * i + k] for k in range(19)]
                out = adjoint(mu, get(u_ref, r, (i,), 3), om_ref[p, block(r), :])
                put_mirrored(lam, out, flip, r, (i,))

        pull(0, even)
        for h in range(2):
            base = h * (BLOCKS // 2)

            def pair(i, carry, base=base):
                r = base + 2 * i
                pull(r + 1, odd)
                stream(r)
                turn(r, even)
                pull(jnp.minimum(r + 2, BLOCKS - 1), even)
                stream(r + 1)
                turn(r + 1, odd)
                moved(flat, final, sem, r).start()
                moved(flat, final, sem, r + 1).start()
                return carry

            lax.fori_loop(0, BLOCKS // 4, pair, 0)
            for i, p in enumerate(INNER):
                copy(i, p, h).start()
        edge_last(ready_n, other, got, om_ref, un_ref, grad, hold, near_sem, NEAR, flip)
        for h in range(2):
            for i, p in enumerate(INNER):
                copy(i, p, h).wait()
        loop(lambda r: moved(flat, final, sem, r).wait())

    by_side(run)


def edge_last(ready, other, got, om_ref, u_ref, grad, hold, sem, p, flip):
    def copy(i):
        rows = pl.ds(i * PIECE * 8, PIECE * 8)
        return pltpu.make_async_copy(
            hold.at[:, rows, :], grad.at[:, rows, place(flip, p), :], sem.at[i]
        )

    receive(other, got, p, -1)
    for i in range(BLOCKS // PIECE):
        for r in range(i * PIECE, (i + 1) * PIECE):
            mu = edge_values(ready, got, p, r, -1)
            out = adjoint(mu, get(u_ref, r, count=3), om_ref[p, block(r), :])
            put_mirrored(hold, out, flip, r)
        copy(i).start()
    for i in range(BLOCKS // PIECE):
        copy(i).wait()


def far_last(ready, other, om_ref, u_ref, partial, grad, hold, sem, got):
    by_side(
        lambda flip: edge_last(ready, other, got, om_ref, u_ref, grad, hold, sem, FAR, flip)
    )


INSIDE = pl.BlockSpec(memory_space=pltpu.VMEM)
OUTSIDE = pl.BlockSpec(memory_space=pltpu.HBM)
STEP, PIECE = 2, 2
INNERS = (19, 2, ROWS, LANES)
PLANE = (19, ROWS, LANES)
RELAX = (PLANES, ROWS, LANES)
CROSS = (5, ROWS, LANES)
NATIVE = (19, PLANES * ROWS, LANES)
RESULT = (19, ROWS, PLANES, LANES)
SEMS = pltpu.SemaphoreType.DMA((BLOCKS,))
GOT = [pltpu.VMEM(CROSS, F32)]


def kernel(body, outs, scratch=(), aliases=None):
    def call(*args):
        args = [x if isinstance(x, tuple) else (x, 1) for x in args]
        return pl.pallas_call(
            body,
            in_specs=[INSIDE if inside else OUTSIDE for _, inside in args],
            out_specs=[INSIDE if inside else OUTSIDE for _, inside in outs],
            out_shape=[
                pltpu.VMEM(s, F32) if inside else jax.ShapeDtypeStruct(s, F32) for s, inside in outs
            ],
            scratch_shapes=list(scratch),
            input_output_aliases=aliases or {},
            compiler_params=pltpu.CompilerParams(vmem_limit_bytes=12 * 2**20),
            name=body.__name__,
        )(
            *[
                pltpu.with_memory_space_constraint(x, pltpu.VMEM if inside else pltpu.HBM)
                for x, inside in args
            ]
        )

    return call


def local(populations, relax_class, cotangent):
    count = lax.axis_size("gx")
    near_pairs = [(i, i ^ 1) for i in range(count)]
    far_pairs = [(i, (i + 1 if i % 2 else i - 1) % count) for i in range(count)]

    def exchange(far, near):
        near = lax.ppermute(near, "gx", near_pairs)
        return lax.ppermute(far, "gx", far_pairs), near

    def to_native(x):
        lead = x.shape[:-2]
        x = x.reshape(lead + (PLANES, ROWS, LANES))
        return jnp.swapaxes(x, -3, -2).reshape(lead + (PLANES * ROWS, LANES))

    pops, classes, cot = to_native(populations), to_native(relax_class), to_native(cotangent)
    inners, plane, cross = (INNERS, 1), (PLANE, 1), (CROSS, 1)
    speed, speeds, state = ((3, ROWS, LANES), 1), ((3, 2, ROWS, LANES), 1), ((4, ROWS, LANES), 1)
    om, post_f, post_n, u0_f, u0_n, far, near = kernel(
        first_edges,
        [(RELAX, 1), plane, plane, speed, speed, cross, cross],
        [pltpu.VMEM(PLANE, F32), pltpu.VMEM(PLANE, F32), pltpu.VMEM(classes.shape, jnp.int32)]
        + [SEMS, SEMS, pltpu.SemaphoreType.DMA],
    )((pops.reshape(RESULT), 0), (classes, 0))
    cot, far, near = lax.optimization_barrier((cot, far, near))
    far, near = exchange(far, near)
    cot_f, cot_i, cot_n, cfar, cnear = kernel(cotangent_planes, [plane, inners, plane, cross, cross])(
        cot
    )
    cfar, cnear = exchange(cfar, cnear)
    post_i, u0_i = kernel(first_inner, [inners, speeds])(pops, om)
    inner = kernel(forward_inner, [inners, speeds, plane, plane])

    post_i, u1_i, ready_f, ready_n = inner(post_f, post_i, post_n, om)
    post_f, post_n, u1_f, u1_n, far, near = kernel(
        forward_edges, [plane, plane, speed, speed, cross, cross], GOT + GOT
    )(ready_f, ready_n, far, near, om)
    far, near = exchange(far, near)
    post_i, u2_i, ready_f, ready_n = inner(post_f, post_i, post_n, om)
    lam_i, mus_f, mus_n = kernel(adjoint_top, [inners, plane, plane])(
        cot_f, cot_i, cot_n, om, u2_i, cfar, cnear
    )
    turn = [kernel(turn_edge(p), [plane, cross, cross, state]) for p in (FAR, NEAR)]
    lam_n, near, got_n, state_n = turn[1](ready_n, near, om, mus_n)
    lam_f, far, got_f, state_f = turn[0](ready_f, far, om, mus_f)
    far, near = exchange(far, near)
    post_f, post_n, pfar, pnear = kernel(relax_edges, [plane, plane, cross, cross])(
        ready_f, got_f, state_f, ready_n, got_n, state_n, om
    )
    lam_i, ready_f, ready_n = kernel(adjoint_inner, [inners, plane, plane])(
        lam_f, lam_i, lam_n, om, u1_i
    )
    pfar, pnear = exchange(pfar, pnear)
    edge = [kernel(adjoint_edge(p), [plane, cross], GOT) for p in (FAR, NEAR)]
    lam_n, near = edge[1](ready_n, near, om, u1_n)
    lam_f, far = edge[0](ready_f, far, om, u1_f)
    far, near = exchange(far, near)
    quad_sem = pltpu.SemaphoreType.DMA((4,))
    grad, ready_f, final = kernel(
        finish,
        [(RESULT, 0), plane, (NATIVE, 0)],
        [pltpu.VMEM(NATIVE, F32), pltpu.VMEM(PLANE, F32), SEMS, quad_sem, quad_sem]
        + [pltpu.VMEM(INNERS, F32), pltpu.VMEM(PLANE, F32)]
        + [pltpu.VMEM((38, 8, LANES), F32), pltpu.VMEM((38, 8, LANES), F32)]
        + GOT,
    )(lam_f, lam_i, lam_n, om, u0_i, u0_n, near, post_f, post_i, post_n, pfar, pnear)
    (grad,) = kernel(far_last, [(RESULT, 0)], [pltpu.VMEM(PLANE, F32), quad_sem] + GOT, {4: 0})(
        ready_f, far, om, u0_f, (grad, 0)
    )
    final = jnp.swapaxes(final.reshape(19, ROWS, PLANES, LANES), 1, 2)
    return final.reshape(populations.shape), jnp.swapaxes(grad, 1, 2).reshape(populations.shape)


def solution(mesh):
    return jax.shard_map(
        local,
        mesh=mesh,
        in_specs=(
            P(None, ("groups", "gx"), None),
            P(("groups", "gx"), None),
            P(None, ("groups", "gx"), None),
        ),
        out_specs=(P(None, ("groups", "gx"), None), P(None, ("groups", "gx"), None)),
        check_vma=False,
    )
```

```python
import jax
import jax.numpy as jnp
from jax import lax
from jax.experimental import pallas as pl
from jax.experimental.pallas import tpu as pltpu
from jax.sharding import PartitionSpec as P

PLANES, ROWS, LANES, BLOCKS = 4, 64, 128, 8
SPEEDS = [
    (0, 0, 0), (1, 0, 0), (-1, 0, 0), (0, 1, 0), (0, -1, 0), (0, 0, 1), (0, 0, -1),
    (1, 1, 0), (-1, -1, 0), (1, -1, 0), (-1, 1, 0), (1, 0, 1), (-1, 0, -1),
    (1, 0, -1), (-1, 0, 1), (0, 1, 1), (0, -1, -1), (0, 1, -1), (0, -1, 1),
]
RATES = [1.0 / 1.0, 1.0 / 1.25, 1.0 / 1.6, 1.0 / 2.4]
MIRROR = [SPEEDS.index((-cx, cy, cz)) for cx, cy, cz in SPEEDS]
PLUS = [k for k in range(19) if SPEEDS[k][0] == 1]
MINUS = [MIRROR[k] for k in PLUS]
F32 = jnp.float32


def iotas():
    lane = lax.broadcasted_iota(jnp.int32, (8, LANES), 1)
    row = lax.broadcasted_iota(jnp.int32, (8, LANES), 0)
    turns = {}
    for turn in (0, 64):
        for cz in (1, -1):
            turns[turn, cz] = ((lane & 64) ^ turn) | ((lane - cz) & 63)
    return {"high": lane >= 64, "top": row == 0, "bottom": row == 7, **turns}


def block(r):
    return pl.ds(r * 8 if isinstance(r, int) else pl.multiple_of(r * 8, 8), 8)


def shifted(ref, index, r, cy, cz, m):
    here = ref[index + (block(r), slice(None))]
    turn = 0
    if cy == 1:
        edge = ref[index + (pl.ds(((r + 7) & 7) * 8 + 7, 1), slice(None))]
        other = jnp.where(m["top"], edge, pltpu.roll(here, 1, 0))
        here, turn = jnp.where(m["high"], other, here), 64
    elif cy == -1:
        edge = ref[index + (pl.ds(((r + 1) & 7) * 8, 1), slice(None))]
        other = jnp.where(m["bottom"], edge, pltpu.roll(here, 7, 0))
        here, turn = jnp.where(m["high"], here, other), 64
    if cz == 0:
        return pltpu.roll(here, turn, 1) if turn else here
    return jnp.take_along_axis(here, m[turn, cz], axis=1)


def moments(f):
    s = [f[k] + f[k + 1] for k in range(1, 19, 2)]
    d = [f[k] - f[k + 1] for k in range(1, 19, 2)]
    rho = f[0] + ((s[0] + s[1]) + (s[2] + s[3])) + ((s[4] + s[5]) + (s[6] + s[7])) + s[8]
    jx = d[0] + ((d[3] + d[4]) + (d[5] + d[6]))
    jy = d[1] + ((d[3] - d[4]) + (d[7] + d[8]))
    jz = d[2] + ((d[5] - d[6]) + (d[7] - d[8]))
    return rho, jx, jy, jz


def along_odd(k, v):
    total = None
    for c, x in zip(SPEEDS[k], v):
        if c:
            total = x if total is None else (total + x if c == 1 else total - x)
    return total


def relaxed(f, rho, u, om):
    keep = 1.0 - om
    wr = om * rho
    shape = 1.0 - 1.5 * (u[0] * u[0] + u[1] * u[1] + u[2] * u[2])
    out = [None] * 19
    out[0] = keep * f[0] + (wr * (1.0 / 3.0)) * shape
    for first, last, w in ((1, 7, 1.0 / 18.0), (7, 19, 1.0 / 36.0)):
        part = wr * w
        base, lin, quad = part * shape, part * 3.0, part * 4.5
        for k in range(first, last, 2):
            a = along_odd(k, u)
            even, odd = base + quad * (a * a), lin * a
            out[k] = keep * f[k] + (even + odd)
            out[k + 1] = keep * f[k + 1] + (even - odd)
    return out


def adjoint(mu, u, om):
    s = [None] + [mu[k] + mu[k + 1] for k in range(1, 19, 2)]
    d = [None] + [mu[k] - mu[k + 1] for k in range(1, 19, 2)]
    a, b = 1.0 / 18.0, 1.0 / 36.0
    s45, s67, s89 = s[4] + s[5], s[6] + s[7], s[8] + s[9]
    xx = a * s[1] + b * (s45 + s67)
    yy = a * s[2] + b * (s45 + s89)
    zz = a * s[3] + b * (s67 + s89)
    m0 = (1.0 / 3.0) * mu[0] + a * ((s[1] + s[2]) + s[3]) + b * ((s45 + s67) + s89)
    xy, xz, yz = b * (s[4] - s[5]), b * (s[6] - s[7]), b * (s[8] - s[9])
    mx = a * d[1] + b * ((d[4] + d[5]) + (d[6] + d[7]))
    my = a * d[2] + b * ((d[4] - d[5]) + (d[8] + d[9]))
    mz = a * d[3] + b * ((d[6] - d[7]) + (d[8] - d[9]))
    vx = xx * u[0] + xy * u[1] + xz * u[2]
    vy = xy * u[0] + yy * u[1] + yz * u[2]
    vz = xz * u[0] + yz * u[1] + zz * u[2]
    uu = u[0] * u[0] + u[1] * u[1] + u[2] * u[2]
    rho_part = om * (m0 + 1.5 * (m0 * uu) - 4.5 * (u[0] * vx + u[1] * vy + u[2] * vz))
    om3 = 3.0 * om
    flow = [
        om3 * (mx + 3.0 * vx - u[0] * m0),
        om3 * (my + 3.0 * vy - u[1] * m0),
        om3 * (mz + 3.0 * vz - u[2] * m0),
    ]
    keep = 1.0 - om
    out = [None] * 19
    out[0] = keep * mu[0] + rho_part
    for k in range(1, 19, 2):
        g = along_odd(k, flow)
        out[k] = keep * mu[k] + (rho_part + g)
        out[k + 1] = keep * mu[k + 1] + (rho_part - g)
    return out


FAR, NEAR, INNER = 0, PLANES - 1, (1, 2)


def plane_of(parts, p):
    far, inner, near = parts
    return (far, ()) if p == FAR else (near, ()) if p == NEAR else (inner, (INNER.index(p),))


def pull_local(parts, p, r, sign, m):
    out = [None] * 19
    for k in range(19):
        cx, cy, cz = (sign * c for c in SPEEDS[k])
        if 0 <= p - cx < PLANES:
            ref, i = plane_of(parts, p - cx)
            out[k] = shifted(ref, (k,) + i, r, cy, cz, m)
    return out


def crossing(p, sign):
    return (PLUS, MINUS)[(sign == 1) != (p == FAR)]


def pull_remote(other, out, p, r, sign, m):
    for i, k in enumerate(crossing(p, sign)):
        out[k] = shifted(other, (i,), r, sign * SPEEDS[k][1], sign * SPEEDS[k][2], m)
    return out


def put(ref, values, r, i=()):
    for k, value in enumerate(values):
        if value is not None:
            ref[(k,) + i + (block(r), slice(None))] = value


def get(ref, r, i=(), count=19, missing=()):
    return [
        None if k in missing else ref[(k,) + i + (block(r), slice(None))] for k in range(count)
    ]


def put_crossing(ref, values, p, r, sign):
    put(ref, [values[k] for k in crossing(p, -sign)], r)


def state_of(f):
    rho, jx, jy, jz = moments(f)
    inv = 1.0 / rho
    return rho, [jx * inv, jy * inv, jz * inv]


def by_side(run):
    side = lax.rem(lax.axis_index("gx"), 2)
    for flip in (0, 1):
        pl.when(side == flip)(lambda flip=flip: run(flip))


def native(flip, k, p, r):
    return mirrored(flip, k), pl.ds(r * (8 * PLANES) + place(flip, p), 8, stride=PLANES)


def mirrored(flip, k):
    return MIRROR[k] if flip else k


def place(flip, p):
    return PLANES - 1 - p if flip else p


def get_native(ref, flip, p, r):
    out = []
    for k in range(19):
        kk, rows = native(flip, k, p, r)
        out.append(ref[kk, rows, :])
    return out


def put_native(ref, values, flip, p, r):
    for k in range(19):
        kk, rows = native(flip, k, p, r)
        ref[kk, rows, :] = values[k]


def put_mirrored(hold, values, flip, r, i=()):
    for k in range(19):
        hold[(mirrored(flip, k),) + i + (block(r), slice(None))] = values[k]


def loop(body, step=1):
    def steps(r, carry):
        for j in range(step):
            body(r * step + j)
        return carry

    lax.fori_loop(0, BLOCKS // step, steps, 0)


def chunk(ref, r):
    rows = 8 * PLANES
    return ref.at[:, pl.ds(pl.multiple_of(r * rows, rows), rows), :]


def moved(source, target, sem, r):
    return pltpu.make_async_copy(chunk(source, r), chunk(target, r), sem.at[r])


def first_far(pops, classes, om_ref, post, u_ref, out_ref, held, cls_ref, sem, cls_sem):
    fetch = pltpu.make_async_copy(classes, cls_ref, cls_sem)

    def run(flip):
        def copy(r):
            return pltpu.make_async_copy(
                pops.at[:, block(r), place(flip, FAR), :], held.at[:, block(r), :], sem.at[r]
            )

        def body(r):
            for p in range(PLANES):
                cls = cls_ref[native(flip, 0, p, r)[1], :]
                om = jnp.full((8, LANES), RATES[0], F32)
                for entry in range(1, 4):
                    om = jnp.where(cls == entry, RATES[entry], om)
                om_ref[p, block(r), :] = om
            copy(r).wait()
            f = [held[mirrored(flip, k), block(r), :] for k in range(19)]
            rho, u = state_of(f)
            put(u_ref, u, r)
            out = relaxed(f, rho, u, om_ref[FAR, block(r), :])
            put(post, out, r)
            put_crossing(out_ref, out, FAR, r, 1)

        loop(lambda r: copy(r).start())
        fetch.wait()
        loop(body)

    fetch.start()
    by_side(run)


def first_rest(pops, om_ref, post_i, post_n, u_i, u_n, out_ref):
    def run(flip):
        def body(r):
            for p in (*INNER, NEAR):
                f = get_native(pops, flip, p, r)
                rho, u = state_of(f)
                out = relaxed(f, rho, u, om_ref[p, block(r), :])
                if p == NEAR:
                    put(u_n, u, r)
                    put(post_n, out, r)
                    put_crossing(out_ref, out, p, r, 1)
                else:
                    i = (INNER.index(p),)
                    put(u_i, u, r, i)
                    put(post_i, out, r, i)

        loop(body)

    by_side(run)


def cotangent_planes(cot, far, inner, near, far_out, near_out):
    def run(flip):
        def body(r):
            for p in range(PLANES):
                values = get_native(cot, flip, p, r)
                ref, i = plane_of((far, inner, near), p)
                put(ref, values, r, i)
                if p not in INNER:
                    put_crossing(far_out if p == FAR else near_out, values, p, r, -1)

        loop(body)

    by_side(run)


def forward_inner(far, inner, near, om_ref, post, u_ref, ready_f, ready_n):
    parts, m = (far, inner, near), iotas()

    def body(r):
        for i, p in enumerate(INNER):
            f = pull_local(parts, p, r, 1, m)
            rho, u = state_of(f)
            put(u_ref, u, r, (i,))
            put(post, relaxed(f, rho, u, om_ref[p, block(r), :]), r, (i,))
        for p, ready in ((FAR, ready_f), (NEAR, ready_n)):
            put(ready, pull_local(parts, p, r, 1, m), r)

    loop(body, STEP)


def receive(other, got, p, sign):
    m = iotas()
    for r in range(BLOCKS):
        for j, k in enumerate(crossing(p, sign)):
            cy, cz = sign * SPEEDS[k][1], sign * SPEEDS[k][2]
            got[j, block(r), :] = shifted(other, (j,), r, cy, cz, m)


def edge_values(ready, got, p, r, sign):
    values = get(ready, r, missing=crossing(p, sign))
    for j, k in enumerate(crossing(p, sign)):
        values[k] = got[j, block(r), :]
    return values


def forward_edges(
    ready_f, ready_n, far, near, om_ref,
    post_f, post_n, u_f, u_n, out_f, out_n, got_f, got_n,
):
    sides = (
        (FAR, ready_f, far, post_f, u_f, out_f, got_f),
        (NEAR, ready_n, near, post_n, u_n, out_n, got_n),
    )
    for p, _, other, _, _, _, got in sides:
        receive(other, got, p, 1)

    def body(r):
        for p, ready, _, post, u_ref, out_ref, got in sides:
            f = edge_values(ready, got, p, r, 1)
            rho, u = state_of(f)
            put(u_ref, u, r)
            out = relaxed(f, rho, u, om_ref[p, block(r), :])
            put(post, out, r)
            put_crossing(out_ref, out, p, r, 1)

    loop(body)


def adjoint_planes(parts, om_ref, u_ref, lam, r, m):
    for i, p in enumerate(INNER):
        mu = pull_local(parts, p, r, -1, m)
        out = adjoint(mu, get(u_ref, r, (i,), 3), om_ref[p, block(r), :])
        put(lam, out, r, (i,))


def adjoint_inner(far, inner, near, om_ref, u_ref, lam, ready_f, ready_n):
    parts, m = (far, inner, near), iotas()

    def body(r):
        adjoint_planes(parts, om_ref, u_ref, lam, r, m)
        for p, ready in ((FAR, ready_f), (NEAR, ready_n)):
            put(ready, pull_local(parts, p, r, -1, m), r)

    loop(body, STEP)


def adjoint_top(far, inner, near, om_ref, u_ref, other_f, other_n, lam, mus_f, mus_n):
    parts, m = (far, inner, near), iotas()

    def body(r):
        adjoint_planes(parts, om_ref, u_ref, lam, r, m)
        for p, mus, other in ((FAR, mus_f, other_f), (NEAR, mus_n, other_n)):
            put(mus, pull_remote(other, pull_local(parts, p, r, -1, m), p, r, -1, m), r)

    loop(body, STEP)


def adjoint_edge(p):
    def adjoint_edge(ready, other, om_ref, u_ref, lam, out_ref, got):
        receive(other, got, p, -1)

        def body(r):
            mu = edge_values(ready, got, p, r, -1)
            out = adjoint(mu, get(u_ref, r, count=3), om_ref[p, block(r), :])
            put(lam, out, r)
            put_crossing(out_ref, out, p, r, -1)

        loop(body, 2)

    return adjoint_edge


def turn_edge(p):
    def turn_edge(ready, other, om_ref, mus, lam, out_ref, got, state):
        receive(other, got, p, 1)

        def body(r):
            rho, u = state_of(edge_values(ready, got, p, r, 1))
            put(state, u + [rho], r)
            out = adjoint(get(mus, r), u, om_ref[p, block(r), :])
            put(lam, out, r)
            put_crossing(out_ref, out, p, r, -1)

        loop(body, 2)

    return turn_edge


def relax_edges(ready_f, got_f, state_f, ready_n, got_n, state_n, om_ref, post_f, post_n, out_f, out_n):
    def body(r):
        for p, ready, got, state, post, out_ref in (
            (FAR, ready_f, got_f, state_f, post_f, out_f),
            (NEAR, ready_n, got_n, state_n, post_n, out_n),
        ):
            f = edge_values(ready, got, p, r, 1)
            *u, rho = get(state, r, count=4)
            out = relaxed(f, rho, u, om_ref[p, block(r), :])
            put(post, out, r)
            put_crossing(out_ref, out, p, r, 1)

    loop(body)


def finish(
    far, inner, near, om_ref, u_ref, un_ref, other, post_f, post_i, post_n, other_f, other_n,
    grad, ready_f, final, flat, hold, sem, hold_sem, near_sem, lam, ready_n, even, odd, got,
):
    parts, posts, m = (far, inner, near), (post_f, post_i, post_n), iotas()

    def run(flip):
        def copy(i, p, h):
            rows = pl.ds(h * (ROWS // 2), ROWS // 2)
            return pltpu.make_async_copy(
                lam.at[:, i, rows, :], grad.at[:, rows, place(flip, p), :], hold_sem.at[2 * i + h]
            )

        def stream(r):
            for p in range(PLANES):
                f = pull_local(posts, p, r, 1, m)
                if p not in INNER:
                    pull_remote(other_f if p == FAR else other_n, f, p, r, 1, m)
                put_native(flat, f, flip, p, r)

        def pull(r, keep):
            for i, p in enumerate(INNER):
                for k, value in enumerate(pull_local(parts, p, r, -1, m)):
                    keep[19 * i + k] = value
            for p, ready in ((FAR, ready_f), (NEAR, ready_n)):
                put(ready, pull_local(parts, p, r, -1, m), r)

        def turn(r, keep):
            for i, p in enumerate(INNER):
                mu = [keep[19 * i + k] for k in range(19)]
                out = adjoint(mu, get(u_ref, r, (i,), 3), om_ref[p, block(r), :])
                put_mirrored(lam, out, flip, r, (i,))

        pull(0, even)
        for h in range(2):
            base = h * (BLOCKS // 2)

            def pair(i, carry, base=base):
                r = base + 2 * i
                pull(r + 1, odd)
                stream(r)
                turn(r, even)
                pull(jnp.minimum(r + 2, BLOCKS - 1), even)
                stream(r + 1)
                turn(r + 1, odd)
                moved(flat, final, sem, r).start()
                moved(flat, final, sem, r + 1).start()
                return carry

            lax.fori_loop(0, BLOCKS // 4, pair, 0)
            for i, p in enumerate(INNER):
                copy(i, p, h).start()
        edge_last(ready_n, other, got, om_ref, un_ref, grad, hold, near_sem, NEAR, flip)
        for h in range(2):
            for i, p in enumerate(INNER):
                copy(i, p, h).wait()
        loop(lambda r: moved(flat, final, sem, r).wait())

    by_side(run)


def edge_last(ready, other, got, om_ref, u_ref, grad, hold, sem, p, flip):
    def copy(i):
        rows = pl.ds(i * PIECE * 8, PIECE * 8)
        return pltpu.make_async_copy(
            hold.at[:, rows, :], grad.at[:, rows, place(flip, p), :], sem.at[i]
        )

    receive(other, got, p, -1)
    for i in range(BLOCKS // PIECE):
        for r in range(i * PIECE, (i + 1) * PIECE):
            mu = edge_values(ready, got, p, r, -1)
            out = adjoint(mu, get(u_ref, r, count=3), om_ref[p, block(r), :])
            put_mirrored(hold, out, flip, r)
        copy(i).start()
    for i in range(BLOCKS // PIECE):
        copy(i).wait()


def far_last(ready, other, om_ref, u_ref, partial, grad, hold, sem, got):
    by_side(
        lambda flip: edge_last(ready, other, got, om_ref, u_ref, grad, hold, sem, FAR, flip)
    )


INSIDE = pl.BlockSpec(memory_space=pltpu.VMEM)
OUTSIDE = pl.BlockSpec(memory_space=pltpu.HBM)
STEP, PIECE = 2, 2
INNERS = (19, 2, ROWS, LANES)
PLANE = (19, ROWS, LANES)
RELAX = (PLANES, ROWS, LANES)
CROSS = (5, ROWS, LANES)
NATIVE = (19, PLANES * ROWS, LANES)
RESULT = (19, ROWS, PLANES, LANES)
SEMS = pltpu.SemaphoreType.DMA((BLOCKS,))
GOT = [pltpu.VMEM(CROSS, F32)]


def kernel(body, outs, scratch=(), aliases=None):
    def call(*args):
        args = [x if isinstance(x, tuple) else (x, 1) for x in args]
        return pl.pallas_call(
            body,
            in_specs=[INSIDE if inside else OUTSIDE for _, inside in args],
            out_specs=[INSIDE if inside else OUTSIDE for _, inside in outs],
            out_shape=[
                pltpu.VMEM(s, F32) if inside else jax.ShapeDtypeStruct(s, F32) for s, inside in outs
            ],
            scratch_shapes=list(scratch),
            input_output_aliases=aliases or {},
            compiler_params=pltpu.CompilerParams(vmem_limit_bytes=12 * 2**20),
            name=body.__name__,
        )(
            *[
                pltpu.with_memory_space_constraint(x, pltpu.VMEM if inside else pltpu.HBM)
                for x, inside in args
            ]
        )

    return call


def local(populations, relax_class, cotangent):
    count = lax.axis_size("gx")
    near_pairs = [(i, i ^ 1) for i in range(count)]
    far_pairs = [(i, (i + 1 if i % 2 else i - 1) % count) for i in range(count)]

    def exchange(far, near):
        near = lax.ppermute(near, "gx", near_pairs)
        return lax.ppermute(far, "gx", far_pairs), near

    def to_native(x):
        lead = x.shape[:-2]
        x = x.reshape(lead + (PLANES, ROWS, LANES))
        return jnp.swapaxes(x, -3, -2).reshape(lead + (PLANES * ROWS, LANES))

    pops, classes, cot = to_native(populations), to_native(relax_class), to_native(cotangent)
    inners, plane, cross = (INNERS, 1), (PLANE, 1), (CROSS, 1)
    speed, speeds, state = ((3, ROWS, LANES), 1), ((3, 2, ROWS, LANES), 1), ((4, ROWS, LANES), 1)
    om, post_f, u0_f, far = kernel(
        first_far,
        [(RELAX, 1), plane, speed, cross],
        [pltpu.VMEM(PLANE, F32), pltpu.VMEM(classes.shape, jnp.int32), SEMS, pltpu.SemaphoreType.DMA],
    )((pops.reshape(RESULT), 0), (classes, 0))
    cot, far = lax.optimization_barrier((cot, far))
    far = lax.ppermute(far, "gx", far_pairs)
    cot_f, cot_i, cot_n, cfar, cnear = kernel(cotangent_planes, [plane, inners, plane, cross, cross])(
        cot
    )
    pops, cfar, cnear = lax.optimization_barrier((pops, cfar, cnear))
    cfar, cnear = exchange(cfar, cnear)
    post_i, post_n, u0_i, u0_n, near = kernel(first_rest, [inners, plane, speeds, speed, cross])(
        pops, om
    )
    near = lax.ppermute(near, "gx", near_pairs)
    inner = kernel(forward_inner, [inners, speeds, plane, plane])

    post_i, u1_i, ready_f, ready_n = inner(post_f, post_i, post_n, om)
    post_f, post_n, u1_f, u1_n, far, near = kernel(
        forward_edges, [plane, plane, speed, speed, cross, cross], GOT + GOT
    )(ready_f, ready_n, far, near, om)
    far, near = exchange(far, near)
    post_i, u2_i, ready_f, ready_n = inner(post_f, post_i, post_n, om)
    lam_i, mus_f, mus_n = kernel(adjoint_top, [inners, plane, plane])(
        cot_f, cot_i, cot_n, om, u2_i, cfar, cnear
    )
    turn = [kernel(turn_edge(p), [plane, cross, cross, state]) for p in (FAR, NEAR)]
    lam_n, near, got_n, state_n = turn[1](ready_n, near, om, mus_n)
    lam_f, far, got_f, state_f = turn[0](ready_f, far, om, mus_f)
    far, near = exchange(far, near)
    post_f, post_n, pfar, pnear = kernel(relax_edges, [plane, plane, cross, cross])(
        ready_f, got_f, state_f, ready_n, got_n, state_n, om
    )
    lam_i, ready_f, ready_n = kernel(adjoint_inner, [inners, plane, plane])(
        lam_f, lam_i, lam_n, om, u1_i
    )
    pfar, pnear = exchange(pfar, pnear)
    edge = [kernel(adjoint_edge(p), [plane, cross], GOT) for p in (FAR, NEAR)]
    lam_n, near = edge[1](ready_n, near, om, u1_n)
    lam_f, far = edge[0](ready_f, far, om, u1_f)
    far, near = exchange(far, near)
    quad_sem = pltpu.SemaphoreType.DMA((4,))
    grad, ready_f, final = kernel(
        finish,
        [(RESULT, 0), plane, (NATIVE, 0)],
        [pltpu.VMEM(NATIVE, F32), pltpu.VMEM(PLANE, F32), SEMS, quad_sem, quad_sem]
        + [pltpu.VMEM(INNERS, F32), pltpu.VMEM(PLANE, F32)]
        + [pltpu.VMEM((38, 8, LANES), F32), pltpu.VMEM((38, 8, LANES), F32)]
        + GOT,
    )(lam_f, lam_i, lam_n, om, u0_i, u0_n, near, post_f, post_i, post_n, pfar, pnear)
    (grad,) = kernel(far_last, [(RESULT, 0)], [pltpu.VMEM(PLANE, F32), quad_sem] + GOT, {4: 0})(
        ready_f, far, om, u0_f, (grad, 0)
    )
    final = jnp.swapaxes(final.reshape(19, ROWS, PLANES, LANES), 1, 2)
    return final.reshape(populations.shape), jnp.swapaxes(grad, 1, 2).reshape(populations.shape)


def solution(mesh):
    return jax.shard_map(
        local,
        mesh=mesh,
        in_specs=(
            P(None, ("groups", "gx"), None),
            P(("groups", "gx"), None),
            P(None, ("groups", "gx"), None),
        ),
        out_specs=(P(None, ("groups", "gx"), None), P(None, ("groups", "gx"), None)),
        check_vma=False,
    )
```
